32 devices in a mesh: dp: 16 (over z, y, core), tensor: 2 (over x).
Axes of the slice: x: 2, y: 2, z: 4, core: 2. Of those that a mesh axis runs over, the one named last changes fastest.
Arguments:
- hidden: bfloat16 [16, 1024, 28672], P('dp', None, 'tensor'), may hold values from -6 to 6
- grad_out: bfloat16 [16, 1024, 8192], P('dp', None, 'tensor'), may hold values from -30 to 30
- proj_in: bfloat16 [64, 28672], P(None, 'tensor'), may hold values from -0.03125 to 0.03125
- proj_out: bfloat16 [64, 8192], P(None, 'tensor'), may hold values from -0.0625 to 0.0625
Outputs:
- covariance: float32 [4096, 4096], P('dp', 'tensor')
The draws below stay inside these ranges and needn't reach their ends.
All inputs are finite; a program needn't handle non-finite values.
Results may differ from the reference program's by a relative error of at most 0.0003.
Values sent between devices are 32-bit elements; how exact they have to be, the bound alone decides.
A program may use at most 128 MiB of HBM per device.

```python
import math
import jax
import jax.numpy as jnp
from jax import lax

D = 8192
FF = 28672
K = 64
SEQ_LEN = 1024
SEQS = 16
KK = 4096


def draw_grad_out(key, part):
    steps = jnp.arange(SEQS, dtype=jnp.float32) / (SEQS - 1)
    base = jax.random.truncated_normal(key, -6.0, 6.0, (SEQS, SEQ_LEN, D), jnp.float32)
    rising = 3.0 ** steps
    return (base * rising[:, None, None]).astype(jnp.bfloat16)


def shard_levels(own_key, shape, shards, low, largest):
    factor_of = 1.0
    for dim, blocks in shards:
        steps = jax.random.uniform(jax.random.fold_in(jax.random.fold_in(own_key, 6), dim), (blocks,), jnp.float32, low / len(shards), largest / len(shards))
        factor_of = factor_of * jnp.repeat(jnp.exp(steps), shape[dim] // blocks).reshape((-1,) + (1,) * (len(shape) - 1 - dim))
    return factor_of


def bell_draw(own_key, shape, spread, reach, shards=(), kind=jnp.bfloat16):
    array = jax.random.normal(own_key, shape, jnp.float32) * spread
    if len(shards) > 0:
        array = shard_levels(own_key, shape, shards, -0.22, 0.18) * array
    return jnp.clip(array, min=-reach, max=reach).astype(kind)


def setup_inputs(seed: int = 0) -> dict:
    splits = jax.random.split(jax.random.key(seed), 5)
    hidden = bell_draw(splits[0], (SEQS, SEQ_LEN, FF), 1.0, 6.0, ((0, 16), (2, 2)))
    grad_out = draw_grad_out(jax.random.fold_in(splits[4], 71), 0)
    proj_in = bell_draw(splits[2], (K, FF), FF ** -0.5, 0.03125, ((1, 2),))
    proj_out = bell_draw(splits[3], (K, D), D ** -0.5, 0.0625, ((1, 2),))
    return {"hidden": hidden, "grad_out": grad_out, "proj_in": proj_in, "proj_out": proj_out}


def reference(hidden, grad_out, proj_in, proj_out):
    inv_root = 1.0 / math.sqrt(SEQ_LEN)

    def one_sequence(seq_pair):
        seq_hidden, seq_grad = seq_pair
        in_panel = jnp.dot(seq_hidden, proj_in.T, preferred_element_type=jnp.float32)
        out_panel = jnp.dot(seq_grad, proj_out.T, preferred_element_type=jnp.float32)
        outer = jnp.dot(in_panel.T, out_panel, precision=lax.Precision.HIGHEST, preferred_element_type=jnp.float32)
        return (outer * inv_root).reshape(-1)
    seq_grads = lax.map(one_sequence, (hidden, grad_out))
    raw_cov = jnp.dot(seq_grads.T, seq_grads, precision=lax.Precision.HIGHEST, preferred_element_type=jnp.float32) / SEQS
    damping = 0.5 * jnp.sum(seq_grads * seq_grads) / (SEQS * KK)
    return raw_cov + damping * jnp.eye(KK, dtype=jnp.float32)
```

```python
import functools
import math

import jax
import jax.numpy as jnp
from jax import lax
from jax.experimental import pallas as pl
from jax.experimental.pallas import tpu as pltpu
from jax.sharding import PartitionSpec as P

MESH = pl.DeviceIdType.MESH
LANES = 128
AHEAD = 6


def chunk_of(size, largest=1024):
    best = size
    for part in range(LANES, largest + 1, LANES):
        if size % part == 0:
            best = part
    return best


def both_parts(x):
    high = x.astype(jnp.bfloat16)
    low = (x - high.astype(jnp.float32)).astype(jnp.bfloat16)
    return jnp.concatenate([high, low], axis=0)


def contract_last(a, b):
    return lax.dot_general(a, b, (((1,), (1,)), ((), ())), preferred_element_type=jnp.float32)


def grads_kernel(
    n_dp, n_tensor, inv_root,
    hidden, grad_out, proj_in, proj_out,
    cols_out, rows_out, squares_out,
    h_buf, g_buf, wi_buf, wo_buf,
    in_panel, out_panel, out_others, part, flat, mine_in, note, note_in,
    h_sem, g_sem, wi_sem, wo_sem,
    panel_send, panel_recv, part_send, part_recv, cols_send, cols_recv, note_send, note_recv,
):
    dp = lax.axis_index("dp")
    ts = lax.axis_index("tensor")
    h_chunks, _, h_wide = h_buf.shape
    g_chunks, _, g_wide = g_buf.shape
    own_rows = flat.shape[1]
    row_rows = rows_out.shape[1]
    groups = note.shape[0]

    def h_copy(c):
        return pltpu.make_async_copy(
            hidden.at[0, :, pl.ds(pl.multiple_of(c * h_wide, LANES), h_wide)], h_buf.at[c], h_sem.at[c]
        )

    def g_copy(c):
        return pltpu.make_async_copy(
            grad_out.at[0, :, pl.ds(pl.multiple_of(c * g_wide, LANES), g_wide)], g_buf.at[c], g_sem.at[c]
        )

    def wi_copy(c):
        return pltpu.make_async_copy(
            proj_in.at[:, pl.ds(pl.multiple_of(c * h_wide, LANES), h_wide)], wi_buf.at[c], wi_sem.at[c]
        )

    def wo_copy(c):
        return pltpu.make_async_copy(
            proj_out.at[:, pl.ds(pl.multiple_of(c * g_wide, LANES), g_wide)], wo_buf.at[c], wo_sem.at[c]
        )

    copies = [(wo_copy, g_copy, c) for c in range(g_chunks)] + [(wi_copy, h_copy, c) for c in range(h_chunks)]

    def begin(k):
        if k < len(copies):
            weight, data, c = copies[k]
            weight(c).start()
            data(c).start()

    for k in range(AHEAD):
        begin(k)

    barrier = pltpu.get_barrier_semaphore()
    n_all = n_dp * n_tensor

    def greet(i, carry):
        other = lax.rem(dp * n_tensor + ts + i, n_all)
        pl.semaphore_signal(
            barrier, inc=1, device_id=(other // n_tensor, lax.rem(other, n_tensor)), device_id_type=MESH
        )
        return carry

    lax.fori_loop(1, n_all, greet, 0)

    for c in range(g_chunks):
        wo_copy(c).wait()
        g_copy(c).wait()
        begin(c + AHEAD)
        term = contract_last(wo_buf[c], g_buf[c])
        if c == 0:
            out_panel[...] = term
        else:
            out_panel[...] += term

    pl.semaphore_wait(barrier, n_all - 1)

    def panel_copy(i):
        return pltpu.make_async_remote_copy(
            src_ref=out_panel,
            dst_ref=out_others.at[i - 1],
            send_sem=panel_send.at[i - 1],
            recv_sem=panel_recv.at[i - 1],
            device_id=(dp, lax.rem(ts + i, n_tensor)),
            device_id_type=MESH,
        )

    for i in range(1, n_tensor):
        panel_copy(i).start()

    for c in range(h_chunks):
        wi_copy(c).wait()
        h_copy(c).wait()
        begin(g_chunks + c + AHEAD)
        term = contract_last(wi_buf[c], h_buf[c])
        if c == 0:
            in_panel[...] = term
        else:
            in_panel[...] += term

    for i in range(1, n_tensor):
        panel_copy(i).wait()

    total = out_panel[...]
    for i in range(1, n_tensor):
        total = total + out_others[i - 1]
    width = in_panel.shape[0]
    products = contract_last(both_parts(in_panel[...]), both_parts(total))
    sums = products[:width, :width] + products[:width, width:] + products[width:, :width]
    part[...] = sums * inv_root
    even = part[pl.ds(0, width // 2, 2), :]
    odd = part[pl.ds(1, width // 2, 2), :]
    whole = jnp.concatenate([even, odd], axis=1)
    for j in range(n_tensor):
        flat[j] = whole[j * own_rows:(j + 1) * own_rows]

    def part_copy(i):
        to = lax.rem(ts + i, n_tensor)
        return pltpu.make_async_remote_copy(
            src_ref=flat.at[to],
            dst_ref=mine_in.at[i - 1],
            send_sem=part_send.at[i - 1],
            recv_sem=part_recv.at[i - 1],
            device_id=(dp, to),
            device_id_type=MESH,
        )

    for i in range(1, n_tensor):
        part_copy(i).start()
    for i in range(1, n_tensor):
        part_copy(i).wait()
    mine = flat[ts]
    for i in range(1, n_tensor):
        mine = mine + mine_in[i - 1]
    cols_out[0] = mine
    square = jnp.sum(mine * mine)
    for k in range(groups):
        note[k, :row_rows] = mine[k * row_rows:(k + 1) * row_rows]
        note[k, row_rows:] = jnp.full((note.shape[1] - row_rows, LANES), square, jnp.float32)

    def cols_copy(i):
        return pltpu.make_async_remote_copy(
            src_ref=cols_out.at[0],
            dst_ref=cols_out.at[i],
            send_sem=cols_send.at[i],
            recv_sem=cols_recv.at[i],
            device_id=(lax.rem(dp + i, n_dp), ts),
            device_id_type=MESH,
        )

    def note_copy(j, i):
        to = lax.rem(dp + i, n_dp)
        return pltpu.make_async_remote_copy(
            src_ref=note.at[lax.rem(to, groups)],
            dst_ref=note_in.at[j - 1, i],
            send_sem=note_send.at[j - 1, i],
            recv_sem=note_recv.at[j - 1, i],
            device_id=(to, lax.rem(ts + j, n_tensor)),
            device_id_type=MESH,
        )

    def start_cols(i, carry):
        cols_copy(i).start()
        return carry

    def wait_cols(i, carry):
        cols_copy(i).wait()
        return carry

    lax.fori_loop(1, n_dp, start_cols, 0)
    for j in range(1, n_tensor):
        def start_notes(i, carry):
            note_copy(j, i).start()
            return carry

        lax.fori_loop(0, n_dp, start_notes, 0)
    lax.fori_loop(1, n_dp, wait_cols, 0)
    for j in range(1, n_tensor):
        def wait_notes(i, carry):
            note_copy(j, i).wait()
            return carry

        lax.fori_loop(0, n_dp, wait_notes, 0)

    owner = dp // groups
    first = lax.rem(dp, groups)
    for k in range(groups):
        @pl.when(jnp.logical_and(owner == ts, first == k))
        def _():
            rows_out[...] = cols_out[:, k * row_rows:(k + 1) * row_rows]

    squares = jnp.sum(cols_out[...] * cols_out[...])
    for j in range(1, n_tensor):
        @pl.when(owner == lax.rem(ts + n_tensor - j, n_tensor))
        def _():
            rows_out[...] = note_in[j - 1, :, :row_rows]

    others = jnp.zeros((1, LANES), jnp.float32)
    for j in range(1, n_tensor):
        others = others + jnp.sum(note_in[j - 1, :, row_rows], axis=0, keepdims=True)
    squares_out[...] = jnp.broadcast_to(others + squares, squares_out.shape)


def covariance_kernel(n_dp, n_tensor, seqs, total_len, cols, rows, squares, out):
    dp = lax.axis_index("dp")
    ts = lax.axis_index("tensor")
    height, wide = out.shape
    step = pl.program_id(0)
    row_rows = height // LANES
    col_rows = cols.shape[0] // seqs
    here = wide // LANES
    row_tiles = [rows[pl.ds(k, seqs, row_rows), :] for k in range(row_rows)]
    col_tiles = [cols[pl.ds(step * here + k, seqs, col_rows), :] for k in range(here)]
    left = jnp.concatenate(row_tiles, axis=1) * (1.0 / seqs)
    right = jnp.concatenate(col_tiles, axis=1)
    left_hi = left.astype(jnp.bfloat16).astype(jnp.float32)
    left_lo = left - left_hi
    right_hi = right.astype(jnp.bfloat16).astype(jnp.float32)
    right_lo = right - right_hi
    a = jnp.concatenate([left_hi, left_lo, left_hi], axis=0).T.astype(jnp.bfloat16)
    b = jnp.concatenate([right_hi, right_hi, right_lo], axis=0).astype(jnp.bfloat16)
    raw = jnp.dot(a, b, preferred_element_type=jnp.float32)
    damping = squares[0, 0] * (0.5 / (seqs * total_len))
    row_ids = dp * height + lax.broadcasted_iota(jnp.int32, out.shape, 0)
    col_begin = ts * (cols.shape[0] // seqs * LANES) + step * wide
    col_ids = col_begin + lax.broadcasted_iota(jnp.int32, out.shape, 1)
    out[...] = raw + jnp.where(row_ids == col_ids, damping, jnp.float32(0.0))


def shards(n_dp, n_tensor, hidden, grad_out, proj_in, proj_out):
    seqs_here, length, units = hidden.shape
    assert seqs_here == 1
    feats = grad_out.shape[2]
    width = proj_in.shape[0]
    total_len = width * width
    flat_rows = total_len // LANES
    own_rows = flat_rows // n_tensor
    row_rows = flat_rows // n_dp
    groups = own_rows // row_rows
    assert groups * row_rows == own_rows and groups * n_tensor == n_dp
    h_wide, g_wide = chunk_of(units), chunk_of(feats)
    h_chunks, g_chunks = units // h_wide, feats // g_wide
    peers = max(n_tensor - 1, 1)
    note_rows = row_rows + 1
    f32, bf16 = jnp.float32, jnp.bfloat16
    vmem = pl.BlockSpec(memory_space=pltpu.VMEM)
    anywhere = pl.BlockSpec(memory_space=pl.ANY)
    dma = pltpu.SemaphoreType.DMA
    cols, rows, squares = pl.pallas_call(
        functools.partial(grads_kernel, n_dp, n_tensor, 1.0 / math.sqrt(length)),
        out_shape=(
            jax.ShapeDtypeStruct((n_dp, own_rows, LANES), f32),
            jax.ShapeDtypeStruct((n_dp, row_rows, LANES), f32),
            jax.ShapeDtypeStruct((8, LANES), f32),
        ),
        in_specs=[anywhere] * 4,
        out_specs=(vmem, vmem, vmem),
        scratch_shapes=[
            pltpu.VMEM((h_chunks, length, h_wide), bf16),
            pltpu.VMEM((g_chunks, length, g_wide), bf16),
            pltpu.VMEM((h_chunks, width, h_wide), bf16),
            pltpu.VMEM((g_chunks, width, g_wide), bf16),
            pltpu.VMEM((width, length), f32),
            pltpu.VMEM((width, length), f32),
            pltpu.VMEM((peers, width, length), f32),
            pltpu.VMEM((width, width), f32),
            pltpu.VMEM((n_tensor, own_rows, LANES), f32),
            pltpu.VMEM((peers, own_rows, LANES), f32),
            pltpu.VMEM((groups, note_rows, LANES), f32),
            pltpu.VMEM((peers, n_dp, note_rows, LANES), f32),
            dma((h_chunks,)),
            dma((g_chunks,)),
            dma((h_chunks,)),
            dma((g_chunks,)),
            dma((peers,)),
            dma((peers,)),
            dma((peers,)),
            dma((peers,)),
            dma((n_dp,)),
            dma((n_dp,)),
            dma((peers, n_dp)),
            dma((peers, n_dp)),
        ],
        compiler_params=pltpu.CompilerParams(
            collective_id=0, has_side_effects=True, vmem_limit_bytes=56 * 1024 * 1024
        ),
        cost_estimate=pl.CostEstimate(
            flops=2 * length * width * (units + feats),
            bytes_accessed=2 * (length + width) * (units + feats),
            transcendentals=0,
        ),
        name="projected_grads",
    )(hidden, grad_out, proj_in, proj_out)
    height, wide = total_len // n_dp, total_len // n_tensor
    block = min(wide, 512)
    return pl.pallas_call(
        functools.partial(covariance_kernel, n_dp, n_tensor, n_dp, total_len),
        out_shape=jax.ShapeDtypeStruct((height, wide), f32),
        grid=(wide // block,),
        in_specs=[vmem] * 3,
        out_specs=pl.BlockSpec((height, block), lambda i: (0, i)),
        name="covariance",
    )(
        cols.reshape(n_dp * own_rows, LANES),
        rows.reshape(n_dp * row_rows, LANES),
        squares,
    )


def solution(mesh):
    placed = (
        P("dp", None, "tensor"),
        P("dp", None, "tensor"),
        P(None, "tensor"),
        P(None, "tensor"),
    )
    return jax.shard_map(
        functools.partial(shards, mesh.shape["dp"], mesh.shape["tensor"]),
        mesh=mesh, in_specs=placed, out_specs=P("dp", "tensor"), check_vma=False,
    )
```

```python
import functools
import math

import jax
import jax.numpy as jnp
from jax import lax
from jax.experimental import pallas as pl
from jax.experimental.pallas import tpu as pltpu
from jax.sharding import PartitionSpec as P

MESH = pl.DeviceIdType.MESH
LANES = 128
AHEAD = 6


def chunk_of(size, largest=1024):
    best = size
    for part in range(LANES, largest + 1, LANES):
        if size % part == 0:
            best = part
    return best


def both_parts(x):
    high = x.astype(jnp.bfloat16)
    low = (x - high.astype(jnp.float32)).astype(jnp.bfloat16)
    return jnp.concatenate([high, low], axis=0)


def contract_last(a, b):
    return lax.dot_general(a, b, (((1,), (1,)), ((), ())), preferred_element_type=jnp.float32)


def grads_kernel(
    n_dp, n_tensor, inv_root,
    hidden, grad_out, proj_in, proj_out,
    cols_out, rows_out, squares_out,
    h_buf, g_buf, wi_buf, wo_buf, tokens,
    in_panel, out_panel, out_others, part, flat, mine_in, note, note_in,
    h_sem, g_sem, wi_sem, wo_sem,
    panel_send, panel_recv, part_send, part_recv, cols_send, cols_recv, note_send, note_recv,
):
    dp = lax.axis_index("dp")
    ts = lax.axis_index("tensor")
    h_chunks, _, h_wide = h_buf.shape
    g_chunks, _, g_wide = g_buf.shape
    own_rows = flat.shape[1]
    row_rows = rows_out.shape[1]
    groups = note.shape[0]

    def h_copy(c):
        return pltpu.make_async_copy(
            hidden.at[0, :, pl.ds(pl.multiple_of(c * h_wide, LANES), h_wide)], h_buf.at[c], h_sem.at[c]
        )

    def g_copy(c):
        return pltpu.make_async_copy(
            grad_out.at[0, :, pl.ds(pl.multiple_of(c * g_wide, LANES), g_wide)], g_buf.at[c], g_sem.at[c]
        )

    def wi_copy(c):
        return pltpu.make_async_copy(
            proj_in.at[:, pl.ds(pl.multiple_of(c * h_wide, LANES), h_wide)], wi_buf.at[c], wi_sem.at[c]
        )

    def wo_copy(c):
        return pltpu.make_async_copy(
            proj_out.at[:, pl.ds(pl.multiple_of(c * g_wide, LANES), g_wide)], wo_buf.at[c], wo_sem.at[c]
        )

    copies = [(wo_copy, g_copy, c) for c in range(g_chunks)] + [(wi_copy, h_copy, c) for c in range(h_chunks)]

    def begin(k):
        if k < len(copies):
            weight, data, c = copies[k]
            weight(c).start()
            data(c).start()

    for k in range(AHEAD):
        begin(k)

    barrier = pltpu.get_barrier_semaphore()
    n_all = n_dp * n_tensor

    def greet(i, carry):
        other = lax.rem(dp * n_tensor + ts + i, n_all)
        pl.semaphore_signal(
            barrier, inc=1, device_id=(other // n_tensor, lax.rem(other, n_tensor)), device_id_type=MESH
        )
        return carry

    lax.fori_loop(1, n_all, greet, 0)

    for c in range(g_chunks):
        wo_copy(c).wait()
        g_copy(c).wait()
        begin(c + AHEAD)
        term = contract_last(g_buf[c], wo_buf[c])
        if c == 0:
            tokens[...] = term
        else:
            tokens[...] += term
    out_panel[...] = tokens[...].T

    pl.semaphore_wait(barrier, n_all - 1)

    def panel_copy(i):
        return pltpu.make_async_remote_copy(
            src_ref=out_panel,
            dst_ref=out_others.at[i - 1],
            send_sem=panel_send.at[i - 1],
            recv_sem=panel_recv.at[i - 1],
            device_id=(dp, lax.rem(ts + i, n_tensor)),
            device_id_type=MESH,
        )

    for i in range(1, n_tensor):
        panel_copy(i).start()

    for c in range(h_chunks):
        wi_copy(c).wait()
        h_copy(c).wait()
        begin(g_chunks + c + AHEAD)
        term = contract_last(h_buf[c], wi_buf[c])
        if c == 0:
            tokens[...] = term
        else:
            tokens[...] += term
    in_panel[...] = tokens[...].T

    for i in range(1, n_tensor):
        panel_copy(i).wait()

    total = out_panel[...]
    for i in range(1, n_tensor):
        total = total + out_others[i - 1]
    width = in_panel.shape[0]
    products = contract_last(both_parts(in_panel[...]), both_parts(total))
    sums = products[:width, :width] + products[:width, width:] + products[width:, :width]
    part[...] = sums * inv_root
    even = part[pl.ds(0, width // 2, 2), :]
    odd = part[pl.ds(1, width // 2, 2), :]
    whole = jnp.concatenate([even, odd], axis=1)
    for j in range(n_tensor):
        flat[j] = whole[j * own_rows:(j + 1) * own_rows]

    def part_copy(i):
        to = lax.rem(ts + i, n_tensor)
        return pltpu.make_async_remote_copy(
            src_ref=flat.at[to],
            dst_ref=mine_in.at[i - 1],
            send_sem=part_send.at[i - 1],
            recv_sem=part_recv.at[i - 1],
            device_id=(dp, to),
            device_id_type=MESH,
        )

    for i in range(1, n_tensor):
        part_copy(i).start()
    for i in range(1, n_tensor):
        part_copy(i).wait()
    mine = flat[ts]
    for i in range(1, n_tensor):
        mine = mine + mine_in[i - 1]
    cols_out[0] = mine
    square = jnp.sum(mine * mine)
    for k in range(groups):
        note[k, :row_rows] = mine[k * row_rows:(k + 1) * row_rows]
        note[k, row_rows:] = jnp.full((note.shape[1] - row_rows, LANES), square, jnp.float32)

    def cols_copy(i):
        return pltpu.make_async_remote_copy(
            src_ref=cols_out.at[0],
            dst_ref=cols_out.at[i],
            send_sem=cols_send.at[i],
            recv_sem=cols_recv.at[i],
            device_id=(lax.rem(dp + i, n_dp), ts),
            device_id_type=MESH,
        )

    def note_copy(j, i):
        to = lax.rem(dp + i, n_dp)
        return pltpu.make_async_remote_copy(
            src_ref=note.at[lax.rem(to, groups)],
            dst_ref=note_in.at[j - 1, i],
            send_sem=note_send.at[j - 1, i],
            recv_sem=note_recv.at[j - 1, i],
            device_id=(to, lax.rem(ts + j, n_tensor)),
            device_id_type=MESH,
        )

    def start_cols(i, carry):
        cols_copy(i).start()
        return carry

    def wait_cols(i, carry):
        cols_copy(i).wait()
        return carry

    lax.fori_loop(1, n_dp, start_cols, 0)
    for j in range(1, n_tensor):
        def start_notes(i, carry):
            note_copy(j, i).start()
            return carry

        lax.fori_loop(0, n_dp, start_notes, 0)
    lax.fori_loop(1, n_dp, wait_cols, 0)
    for j in range(1, n_tensor):
        def wait_notes(i, carry):
            note_copy(j, i).wait()
            return carry

        lax.fori_loop(0, n_dp, wait_notes, 0)

    owner = dp // groups
    first = lax.rem(dp, groups)
    for k in range(groups):
        @pl.when(jnp.logical_and(owner == ts, first == k))
        def _():
            rows_out[...] = cols_out[:, k * row_rows:(k + 1) * row_rows]

    squares = jnp.sum(cols_out[...] * cols_out[...])
    for j in range(1, n_tensor):
        @pl.when(owner == lax.rem(ts + n_tensor - j, n_tensor))
        def _():
            rows_out[...] = note_in[j - 1, :, :row_rows]

    others = jnp.zeros((1, LANES), jnp.float32)
    for j in range(1, n_tensor):
        others = others + jnp.sum(note_in[j - 1, :, row_rows], axis=0, keepdims=True)
    squares_out[...] = jnp.broadcast_to(others + squares, squares_out.shape)


def covariance_kernel(n_dp, n_tensor, seqs, total_len, cols, rows, squares, out):
    dp = lax.axis_index("dp")
    ts = lax.axis_index("tensor")
    height, wide = out.shape
    step = pl.program_id(0)
    row_rows = height // LANES
    col_rows = cols.shape[0] // seqs
    here = wide // LANES
    row_tiles = [rows[pl.ds(k, seqs, row_rows), :] for k in range(row_rows)]
    col_tiles = [cols[pl.ds(step * here + k, seqs, col_rows), :] for k in range(here)]
    left = jnp.concatenate(row_tiles, axis=1) * (1.0 / seqs)
    right = jnp.concatenate(col_tiles, axis=1)
    left_hi = left.astype(jnp.bfloat16).astype(jnp.float32)
    left_lo = left - left_hi
    right_hi = right.astype(jnp.bfloat16).astype(jnp.float32)
    right_lo = right - right_hi
    a = jnp.concatenate([left_hi, left_lo, left_hi], axis=0).T.astype(jnp.bfloat16)
    b = jnp.concatenate([right_hi, right_hi, right_lo], axis=0).astype(jnp.bfloat16)
    raw = jnp.dot(a, b, preferred_element_type=jnp.float32)
    damping = squares[0, 0] * (0.5 / (seqs * total_len))
    row_ids = dp * height + lax.broadcasted_iota(jnp.int32, out.shape, 0)
    col_begin = ts * (cols.shape[0] // seqs * LANES) + step * wide
    col_ids = col_begin + lax.broadcasted_iota(jnp.int32, out.shape, 1)
    out[...] = raw + jnp.where(row_ids == col_ids, damping, jnp.float32(0.0))


def shards(n_dp, n_tensor, hidden, grad_out, proj_in, proj_out):
    seqs_here, length, units = hidden.shape
    assert seqs_here == 1
    feats = grad_out.shape[2]
    width = proj_in.shape[0]
    total_len = width * width
    flat_rows = total_len // LANES
    own_rows = flat_rows // n_tensor
    row_rows = flat_rows // n_dp
    groups = own_rows // row_rows
    assert groups * row_rows == own_rows and groups * n_tensor == n_dp
    h_wide, g_wide = chunk_of(units), chunk_of(feats)
    h_chunks, g_chunks = units // h_wide, feats // g_wide
    peers = max(n_tensor - 1, 1)
    note_rows = row_rows + 1
    f32, bf16 = jnp.float32, jnp.bfloat16
    vmem = pl.BlockSpec(memory_space=pltpu.VMEM)
    anywhere = pl.BlockSpec(memory_space=pl.ANY)
    dma = pltpu.SemaphoreType.DMA
    cols, rows, squares = pl.pallas_call(
        functools.partial(grads_kernel, n_dp, n_tensor, 1.0 / math.sqrt(length)),
        out_shape=(
            jax.ShapeDtypeStruct((n_dp, own_rows, LANES), f32),
            jax.ShapeDtypeStruct((n_dp, row_rows, LANES), f32),
            jax.ShapeDtypeStruct((8, LANES), f32),
        ),
        in_specs=[anywhere] * 4,
        out_specs=(vmem, vmem, vmem),
        scratch_shapes=[
            pltpu.VMEM((h_chunks, length, h_wide), bf16),
            pltpu.VMEM((g_chunks, length, g_wide), bf16),
            pltpu.VMEM((h_chunks, width, h_wide), bf16),
            pltpu.VMEM((g_chunks, width, g_wide), bf16),
            pltpu.VMEM((length, width), f32),
            pltpu.VMEM((width, length), f32),
            pltpu.VMEM((width, length), f32),
            pltpu.VMEM((peers, width, length), f32),
            pltpu.VMEM((width, width), f32),
            pltpu.VMEM((n_tensor, own_rows, LANES), f32),
            pltpu.VMEM((peers, own_rows, LANES), f32),
            pltpu.VMEM((groups, note_rows, LANES), f32),
            pltpu.VMEM((peers, n_dp, note_rows, LANES), f32),
            dma((h_chunks,)),
            dma((g_chunks,)),
            dma((h_chunks,)),
            dma((g_chunks,)),
            dma((peers,)),
            dma((peers,)),
            dma((peers,)),
            dma((peers,)),
            dma((n_dp,)),
            dma((n_dp,)),
            dma((peers, n_dp)),
            dma((peers, n_dp)),
        ],
        compiler_params=pltpu.CompilerParams(
            collective_id=0, has_side_effects=True, vmem_limit_bytes=56 * 1024 * 1024
        ),
        cost_estimate=pl.CostEstimate(
            flops=2 * length * width * (units + feats),
            bytes_accessed=2 * (length + width) * (units + feats),
            transcendentals=0,
        ),
        name="projected_grads",
    )(hidden, grad_out, proj_in, proj_out)
    height, wide = total_len // n_dp, total_len // n_tensor
    block = min(wide, 512)
    return pl.pallas_call(
        functools.partial(covariance_kernel, n_dp, n_tensor, n_dp, total_len),
        out_shape=jax.ShapeDtypeStruct((height, wide), f32),
        grid=(wide // block,),
        in_specs=[vmem] * 3,
        out_specs=pl.BlockSpec((height, block), lambda i: (0, i)),
        name="covariance",
    )(
        cols.reshape(n_dp * own_rows, LANES),
        rows.reshape(n_dp * row_rows, LANES),
        squares,
    )


def solution(mesh):
    placed = (
        P("dp", None, "tensor"),
        P("dp", None, "tensor"),
        P(None, "tensor"),
        P(None, "tensor"),
    )
    return jax.shard_map(
        functools.partial(shards, mesh.shape["dp"], mesh.shape["tensor"]),
        mesh=mesh, in_specs=placed, out_specs=P("dp", "tensor"), check_vma=False,
    )
```

```python
import functools
import math

import jax
import jax.numpy as jnp
from jax import lax
from jax.experimental import pallas as pl
from jax.experimental.pallas import tpu as pltpu
from jax.sharding import PartitionSpec as P

MESH = pl.DeviceIdType.MESH
LANES = 128
AHEAD = 6


def chunk_of(size, largest=1024):
    best = size
    for part in range(LANES, largest + 1, LANES):
        if size % part == 0:
            best = part
    return best


def both_parts(x):
    high = x.astype(jnp.bfloat16)
    low = (x - high.astype(jnp.float32)).astype(jnp.bfloat16)
    return jnp.concatenate([high, low], axis=0)


def contract_last(a, b):
    return lax.dot_general(a, b, (((1,), (1,)), ((), ())), preferred_element_type=jnp.float32)


def grads_kernel(
    n_dp, n_tensor, inv_root,
    hidden, grad_out, proj_in, proj_out,
    gathered,
    h_buf, g_buf, wi_buf, wo_buf,
    in_panel, out_panel, out_others, part, flat, flat_others, message,
    h_sem, g_sem, wi_sem, wo_sem,
    panel_send, panel_recv, part_send, part_recv, message_send, message_recv,
):
    dp = lax.axis_index("dp")
    ts = lax.axis_index("tensor")
    h_chunks, _, h_wide = h_buf.shape
    g_chunks, _, g_wide = g_buf.shape
    flat_rows = flat.shape[0]
    own_rows = flat_rows // n_tensor
    row_rows = flat_rows // n_dp
    used = own_rows + row_rows + 1

    def h_copy(c):
        return pltpu.make_async_copy(
            hidden.at[0, :, pl.ds(pl.multiple_of(c * h_wide, LANES), h_wide)], h_buf.at[c], h_sem.at[c]
        )

    def g_copy(c):
        return pltpu.make_async_copy(
            grad_out.at[0, :, pl.ds(pl.multiple_of(c * g_wide, LANES), g_wide)], g_buf.at[c], g_sem.at[c]
        )

    def wi_copy(c):
        return pltpu.make_async_copy(
            proj_in.at[:, pl.ds(pl.multiple_of(c * h_wide, LANES), h_wide)], wi_buf.at[c], wi_sem.at[c]
        )

    def wo_copy(c):
        return pltpu.make_async_copy(
            proj_out.at[:, pl.ds(pl.multiple_of(c * g_wide, LANES), g_wide)], wo_buf.at[c], wo_sem.at[c]
        )

    copies = [(wo_copy, g_copy, c) for c in range(g_chunks)] + [(wi_copy, h_copy, c) for c in range(h_chunks)]

    def begin(k):
        if k < len(copies):
            weight, data, c = copies[k]
            weight(c).start()
            data(c).start()

    for k in range(AHEAD):
        begin(k)

    barrier = pltpu.get_barrier_semaphore()
    n_all = n_dp * n_tensor

    def greet(i, carry):
        other = lax.rem(dp * n_tensor + ts + i, n_all)
        pl.semaphore_signal(
            barrier, inc=1, device_id=(other // n_tensor, lax.rem(other, n_tensor)), device_id_type=MESH
        )
        return carry

    lax.fori_loop(1, n_all, greet, 0)

    for c in range(g_chunks):
        wo_copy(c).wait()
        g_copy(c).wait()
        begin(c + AHEAD)
        term = contract_last(wo_buf[c], g_buf[c])
        if c == 0:
            out_panel[...] = term
        else:
            out_panel[...] += term

    pl.semaphore_wait(barrier, n_all - 1)

    def panel_copy(i):
        return pltpu.make_async_remote_copy(
            src_ref=out_panel,
            dst_ref=out_others.at[i - 1],
            send_sem=panel_send.at[i - 1],
            recv_sem=panel_recv.at[i - 1],
            device_id=(dp, lax.rem(ts + i, n_tensor)),
            device_id_type=MESH,
        )

    for i in range(1, n_tensor):
        panel_copy(i).start()

    for c in range(h_chunks):
        wi_copy(c).wait()
        h_copy(c).wait()
        begin(g_chunks + c + AHEAD)
        term = contract_last(wi_buf[c], h_buf[c])
        if c == 0:
            in_panel[...] = term
        else:
            in_panel[...] += term

    for i in range(1, n_tensor):
        panel_copy(i).wait()

    total = out_panel[...]
    for i in range(1, n_tensor):
        total = total + out_others[i - 1]
    width = in_panel.shape[0]
    products = contract_last(both_parts(in_panel[...]), both_parts(total))
    sums = products[:width, :width] + products[:width, width:] + products[width:, :width]
    part[...] = sums * inv_root
    even = part[pl.ds(0, width // 2, 2), :]
    odd = part[pl.ds(1, width // 2, 2), :]
    flat[...] = jnp.concatenate([even, odd], axis=1)

    def part_copy(i):
        return pltpu.make_async_remote_copy(
            src_ref=flat,
            dst_ref=flat_others.at[i - 1],
            send_sem=part_send.at[i - 1],
            recv_sem=part_recv.at[i - 1],
            device_id=(dp, lax.rem(ts + i, n_tensor)),
            device_id_type=MESH,
        )

    for i in range(1, n_tensor):
        part_copy(i).start()
    for i in range(1, n_tensor):
        part_copy(i).wait()
    grads = flat[...]
    for i in range(1, n_tensor):
        grads = grads + flat_others[i - 1]
    mine = grads[:own_rows]
    for j in range(1, n_tensor):
        mine = jnp.where(ts == j, grads[j * own_rows:(j + 1) * own_rows], mine)
    square = jnp.broadcast_to(jnp.sum(grads * grads), (1, LANES))
    for d in range(n_dp):
        message[d, :own_rows] = mine
        message[d, own_rows:own_rows + row_rows] = grads[d * row_rows:(d + 1) * row_rows]
        message[d, own_rows + row_rows:used] = square

    def message_copy(i):
        to = lax.rem(dp + i, n_dp)
        return pltpu.make_async_remote_copy(
            src_ref=message.at[to, pl.ds(0, used)],
            dst_ref=gathered.at[i, pl.ds(0, used)],
            send_sem=message_send.at[i],
            recv_sem=message_recv.at[i],
            device_id=(to, ts),
            device_id_type=MESH,
        )

    for i in range(1, n_dp):
        message_copy(i).start()
    gathered[0] = message[dp]
    for i in range(1, n_dp):
        message_copy(i).wait()


def covariance_kernel(n_dp, n_tensor, total_len, gathered, out, block_sem, result):
    dp = lax.axis_index("dp")
    ts = lax.axis_index("tensor")
    height, wide = out.shape
    row_rows = height // LANES
    own_rows = wide // LANES
    slot = gathered.shape[0] // n_dp
    blocks, _, block = result.shape
    here = block // LANES

    def high_low(first, count):
        tiles = [gathered[pl.ds(first + k, n_dp, slot), :] for k in range(count)]
        x = jnp.concatenate(tiles, axis=1)
        high = x.astype(jnp.bfloat16).astype(jnp.float32)
        return high, x - high

    left_high, left_low = high_low(own_rows, row_rows)
    left = jnp.concatenate([left_high, left_low, left_high], axis=0) * (1.0 / n_dp)
    left = left.T.astype(jnp.bfloat16)
    squares = jnp.sum(gathered[pl.ds(own_rows + row_rows, n_dp, slot), :], axis=0, keepdims=True)
    damping = squares * (0.5 / (n_dp * total_len))
    diagonal = dp * height - ts * wide

    def block_copy(b):
        return pltpu.make_async_copy(result.at[b], out.at[:, pl.ds(b * block, block)], block_sem.at[b])

    for b in range(blocks):
        right_high, right_low = high_low(b * here, here)
        right = jnp.concatenate([right_high, right_high, right_low], axis=0).astype(jnp.bfloat16)
        result[b] = jnp.dot(left, right, preferred_element_type=jnp.float32)
        for k in range(block // height):
            @pl.when(diagonal == b * block + k * height)
            def _():
                for r in range(row_rows):
                    place = (pl.ds(r * LANES, LANES), pl.ds(k * height + r * LANES, LANES))
                    ids = lax.broadcasted_iota(jnp.int32, (LANES, LANES), 0)
                    same = ids == lax.broadcasted_iota(jnp.int32, (LANES, LANES), 1)
                    result[(b, *place)] += jnp.where(same, damping, jnp.float32(0.0))
        block_copy(b).start()
    for b in range(blocks):
        block_copy(b).wait()


def shards(n_dp, n_tensor, hidden, grad_out, proj_in, proj_out):
    seqs_here, length, units = hidden.shape
    assert seqs_here == 1
    feats = grad_out.shape[2]
    width = proj_in.shape[0]
    total_len = width * width
    flat_rows = total_len // LANES
    own_rows = flat_rows // n_tensor
    row_rows = flat_rows // n_dp
    slot = -(-(own_rows + row_rows + 1) // 8) * 8
    h_wide, g_wide = chunk_of(units), chunk_of(feats)
    h_chunks, g_chunks = units // h_wide, feats // g_wide
    peers = max(n_tensor - 1, 1)
    f32, bf16 = jnp.float32, jnp.bfloat16
    vmem = pl.BlockSpec(memory_space=pltpu.VMEM)
    in_hbm = pl.BlockSpec(memory_space=pltpu.HBM)
    dma = pltpu.SemaphoreType.DMA
    gathered = pl.pallas_call(
        functools.partial(grads_kernel, n_dp, n_tensor, 1.0 / math.sqrt(length)),
        out_shape=jax.ShapeDtypeStruct((n_dp, slot, LANES), f32),
        in_specs=[in_hbm] * 4,
        out_specs=vmem,
        scratch_shapes=[
            pltpu.VMEM((h_chunks, length, h_wide), bf16),
            pltpu.VMEM((g_chunks, length, g_wide), bf16),
            pltpu.VMEM((h_chunks, width, h_wide), bf16),
            pltpu.VMEM((g_chunks, width, g_wide), bf16),
            pltpu.VMEM((width, length), f32),
            pltpu.VMEM((width, length), f32),
            pltpu.VMEM((peers, width, length), f32),
            pltpu.VMEM((width, width), f32),
            pltpu.VMEM((flat_rows, LANES), f32),
            pltpu.VMEM((peers, flat_rows, LANES), f32),
            pltpu.VMEM((n_dp, slot, LANES), f32),
            dma((h_chunks,)),
            dma((g_chunks,)),
            dma((h_chunks,)),
            dma((g_chunks,)),
            dma((peers,)),
            dma((peers,)),
            dma((peers,)),
            dma((peers,)),
            dma((n_dp,)),
            dma((n_dp,)),
        ],
        compiler_params=pltpu.CompilerParams(
            collective_id=0, has_side_effects=True, vmem_limit_bytes=50 * 1024 * 1024
        ),
        cost_estimate=pl.CostEstimate(
            flops=2 * length * width * (units + feats),
            bytes_accessed=2 * (length + width) * (units + feats),
            transcendentals=0,
        ),
        name="projected_grads",
    )(*(pltpu.with_memory_space_constraint(x, pltpu.HBM) for x in (hidden, grad_out, proj_in, proj_out)))
    height, wide = total_len // n_dp, total_len // n_tensor
    block = min(wide, 512)
    return pl.pallas_call(
        functools.partial(covariance_kernel, n_dp, n_tensor, total_len),
        out_shape=jax.ShapeDtypeStruct((height, wide), f32),
        in_specs=[vmem],
        out_specs=pl.BlockSpec(memory_space=pltpu.HBM),
        scratch_shapes=[dma((wide // block,)), pltpu.VMEM((wide // block, height, block), f32)],
        compiler_params=pltpu.CompilerParams(vmem_limit_bytes=16 * 1024 * 1024),
        name="covariance",
    )(gathered.reshape(n_dp * slot, LANES))


def solution(mesh):
    placed = (
        P("dp", None, "tensor"),
        P("dp", None, "tensor"),
        P(None, "tensor"),
        P(None, "tensor"),
    )
    return jax.shard_map(
        functools.partial(shards, mesh.shape["dp"], mesh.shape["tensor"]),
        mesh=mesh, in_specs=placed, out_specs=P("dp", "tensor"), check_vma=False,
    )
```

```python
import functools
import math

import jax
import jax.numpy as jnp
from jax import lax
from jax.experimental import pallas as pl
from jax.experimental.pallas import tpu as pltpu
from jax.sharding import PartitionSpec as P

MESH = pl.DeviceIdType.MESH
LANES = 128
AHEAD = 6


def chunk_of(size, largest=1024):
    best = size
    for part in range(LANES, largest + 1, LANES):
        if size % part == 0:
            best = part
    return best


def groups_of(count, first, last):
    runs, c = [], 0
    while c < count:
        size = 1 if c < first or c >= count - last or c + 1 >= count - last else 2
        runs.append(list(range(c, c + size)))
        c += size
    return runs


def both_parts(x):
    high = x.astype(jnp.bfloat16)
    low = (x - high.astype(jnp.float32)).astype(jnp.bfloat16)
    return jnp.concatenate([high, low], axis=0)


def contract_last(a, b):
    return lax.dot_general(a, b, (((1,), (1,)), ((), ())), preferred_element_type=jnp.float32)


def grads_kernel(
    n_dp, n_tensor, inv_root,
    hidden, grad_out, proj_in, proj_out,
    gathered,
    h_buf, g_buf, wi_buf, wo_buf,
    in_panel, out_panel, out_others, total_parts, part, flat, flat_others, message,
    h_sem, g_sem, wi_sem, wo_sem,
    panel_send, panel_recv, part_send, part_recv, message_send, message_recv,
):
    dp = lax.axis_index("dp")
    ts = lax.axis_index("tensor")
    h_chunks, _, h_wide = h_buf.shape
    g_chunks, _, g_wide = g_buf.shape
    flat_rows = flat.shape[0]
    own_rows = flat_rows // n_tensor
    row_rows = flat_rows // n_dp
    used = own_rows + row_rows + 1

    def h_copy(c):
        return pltpu.make_async_copy(
            hidden.at[0, :, pl.ds(pl.multiple_of(c * h_wide, LANES), h_wide)], h_buf.at[c], h_sem.at[c]
        )

    def g_copy(c):
        return pltpu.make_async_copy(
            grad_out.at[0, :, pl.ds(pl.multiple_of(c * g_wide, LANES), g_wide)], g_buf.at[c], g_sem.at[c]
        )

    def wi_copy(c):
        return pltpu.make_async_copy(
            proj_in.at[:, pl.ds(pl.multiple_of(c * h_wide, LANES), h_wide)], wi_buf.at[c], wi_sem.at[c]
        )

    def wo_copy(c):
        return pltpu.make_async_copy(
            proj_out.at[:, pl.ds(pl.multiple_of(c * g_wide, LANES), g_wide)], wo_buf.at[c], wo_sem.at[c]
        )

    copies = [(wo_copy, g_copy, c) for c in range(g_chunks)] + [(wi_copy, h_copy, c) for c in range(h_chunks)]

    def begin(k):
        if k < len(copies):
            weight, data, c = copies[k]
            weight(c).start()
            data(c).start()

    for k in range(AHEAD):
        begin(k)

    barrier = pltpu.get_barrier_semaphore()
    n_all = n_dp * n_tensor

    def greet(i, carry):
        other = lax.rem(dp * n_tensor + ts + i, n_all)
        pl.semaphore_signal(
            barrier, inc=1, device_id=(other // n_tensor, lax.rem(other, n_tensor)), device_id_type=MESH
        )
        return carry

    lax.fori_loop(1, n_all, greet, 0)

    def project(group, weights, data, weight_copy, data_copy, before, panel):
        for c in group:
            weight_copy(c).wait()
            data_copy(c).wait()
            begin(before + c + AHEAD)
        term = contract_last(weights[group[0]], data[group[0]])
        for c in group[1:]:
            term = term + contract_last(weights[c], data[c])
        if group[0] == 0:
            panel[...] = term
        else:
            panel[...] += term

    for group in groups_of(g_chunks, 1, 0):
        project(group, wo_buf, g_buf, wo_copy, g_copy, 0, out_panel)

    pl.semaphore_wait(barrier, n_all - 1)

    def panel_copy(i):
        return pltpu.make_async_remote_copy(
            src_ref=out_panel,
            dst_ref=out_others.at[i - 1],
            send_sem=panel_send.at[i - 1],
            recv_sem=panel_recv.at[i - 1],
            device_id=(dp, lax.rem(ts + i, n_tensor)),
            device_id_type=MESH,
        )

    for i in range(1, n_tensor):
        panel_copy(i).start()

    in_groups = groups_of(h_chunks, 0, 2)
    for group in in_groups[:-1]:
        project(group, wi_buf, h_buf, wi_copy, h_copy, g_chunks, in_panel)
    for i in range(1, n_tensor):
        panel_copy(i).wait()
    total = out_panel[...]
    for i in range(1, n_tensor):
        total = total + out_others[i - 1]
    total_parts[...] = both_parts(total)
    project(in_groups[-1], wi_buf, h_buf, wi_copy, h_copy, g_chunks, in_panel)

    width = in_panel.shape[0]
    products = contract_last(both_parts(in_panel[...]), total_parts[...])
    sums = products[:width, :width] + products[:width, width:] + products[width:, :width]
    part[...] = sums * inv_root
    even = part[pl.ds(0, width // 2, 2), :]
    odd = part[pl.ds(1, width // 2, 2), :]
    flat[...] = jnp.concatenate([even, odd], axis=1)

    def part_copy(i):
        return pltpu.make_async_remote_copy(
            src_ref=flat,
            dst_ref=flat_others.at[i - 1],
            send_sem=part_send.at[i - 1],
            recv_sem=part_recv.at[i - 1],
            device_id=(dp, lax.rem(ts + i, n_tensor)),
            device_id_type=MESH,
        )

    for i in range(1, n_tensor):
        part_copy(i).start()
    for i in range(1, n_tensor):
        part_copy(i).wait()
    grads = flat[...]
    for i in range(1, n_tensor):
        grads = grads + flat_others[i - 1]
    mine = grads[:own_rows]
    for j in range(1, n_tensor):
        mine = jnp.where(ts == j, grads[j * own_rows:(j + 1) * own_rows], mine)
    square = jnp.broadcast_to(jnp.sum(grads * grads), (1, LANES))
    for d in range(n_dp):
        message[d, :own_rows] = mine
        message[d, own_rows:own_rows + row_rows] = grads[d * row_rows:(d + 1) * row_rows]
        message[d, own_rows + row_rows:used] = square

    def message_copy(i):
        to = lax.rem(dp + i, n_dp)
        return pltpu.make_async_remote_copy(
            src_ref=message.at[to, pl.ds(0, used)],
            dst_ref=gathered.at[i, pl.ds(0, used)],
            send_sem=message_send.at[i],
            recv_sem=message_recv.at[i],
            device_id=(to, ts),
            device_id_type=MESH,
        )

    for i in sorted(range(1, n_dp), key=lambda i: -min(i, n_dp - i)):
        message_copy(i).start()
    gathered[0] = message[dp]
    for i in range(1, n_dp):
        message_copy(i).wait()


def covariance_kernel(n_dp, n_tensor, total_len, gathered, out, block_sem, result):
    dp = lax.axis_index("dp")
    ts = lax.axis_index("tensor")
    height, wide = out.shape
    row_rows = height // LANES
    own_rows = wide // LANES
    slot = gathered.shape[0] // n_dp
    blocks, _, block = result.shape
    here = block // LANES

    def high_low(first, count):
        tiles = [gathered[pl.ds(first + k, n_dp, slot), :] for k in range(count)]
        x = jnp.concatenate(tiles, axis=1)
        high = x.astype(jnp.bfloat16).astype(jnp.float32)
        return high, x - high

    left_high, left_low = high_low(own_rows, row_rows)
    left = jnp.concatenate([left_high, left_low, left_high], axis=0) * (1.0 / n_dp)
    left = left.T.astype(jnp.bfloat16)
    squares = jnp.sum(gathered[pl.ds(own_rows + row_rows, n_dp, slot), :], axis=0, keepdims=True)
    damping = squares * (0.5 / (n_dp * total_len))
    diagonal = dp * height - ts * wide

    def block_copy(b):
        return pltpu.make_async_copy(result.at[b], out.at[:, pl.ds(b * block, block)], block_sem.at[b])

    for b in range(blocks):
        right_high, right_low = high_low(b * here, here)
        right = jnp.concatenate([right_high, right_high, right_low], axis=0).astype(jnp.bfloat16)
        result[b] = jnp.dot(left, right, preferred_element_type=jnp.float32)
        for k in range(block // height):
            @pl.when(diagonal == b * block + k * height)
            def _():
                for r in range(row_rows):
                    place = (pl.ds(r * LANES, LANES), pl.ds(k * height + r * LANES, LANES))
                    ids = lax.broadcasted_iota(jnp.int32, (LANES, LANES), 0)
                    same = ids == lax.broadcasted_iota(jnp.int32, (LANES, LANES), 1)
                    result[(b, *place)] += jnp.where(same, damping, jnp.float32(0.0))
        block_copy(b).start()
    for b in range(blocks):
        block_copy(b).wait()


def shards(n_dp, n_tensor, hidden, grad_out, proj_in, proj_out):
    seqs_here, length, units = hidden.shape
    assert seqs_here == 1
    feats = grad_out.shape[2]
    width = proj_in.shape[0]
    total_len = width * width
    flat_rows = total_len // LANES
    own_rows = flat_rows // n_tensor
    row_rows = flat_rows // n_dp
    slot = -(-(own_rows + row_rows + 1) // 8) * 8
    h_wide, g_wide = chunk_of(units), chunk_of(feats)
    h_chunks, g_chunks = units // h_wide, feats // g_wide
    peers = max(n_tensor - 1, 1)
    f32, bf16 = jnp.float32, jnp.bfloat16
    vmem = pl.BlockSpec(memory_space=pltpu.VMEM)
    in_hbm = pl.BlockSpec(memory_space=pltpu.HBM)
    dma = pltpu.SemaphoreType.DMA
    gathered = pl.pallas_call(
        functools.partial(grads_kernel, n_dp, n_tensor, 1.0 / math.sqrt(length)),
        out_shape=jax.ShapeDtypeStruct((n_dp, slot, LANES), f32),
        in_specs=[in_hbm] * 4,
        out_specs=vmem,
        scratch_shapes=[
            pltpu.VMEM((h_chunks, length, h_wide), bf16),
            pltpu.VMEM((g_chunks, length, g_wide), bf16),
            pltpu.VMEM((h_chunks, width, h_wide), bf16),
            pltpu.VMEM((g_chunks, width, g_wide), bf16),
            pltpu.VMEM((width, length), f32),
            pltpu.VMEM((width, length), f32),
            pltpu.VMEM((peers, width, length), f32),
            pltpu.VMEM((2 * width, length), bf16),
            pltpu.VMEM((width, width), f32),
            pltpu.VMEM((flat_rows, LANES), f32),
            pltpu.VMEM((peers, flat_rows, LANES), f32),
            pltpu.VMEM((n_dp, slot, LANES), f32),
            dma((h_chunks,)),
            dma((g_chunks,)),
            dma((h_chunks,)),
            dma((g_chunks,)),
            dma((peers,)),
            dma((peers,)),
            dma((peers,)),
            dma((peers,)),
            dma((n_dp,)),
            dma((n_dp,)),
        ],
        compiler_params=pltpu.CompilerParams(
            collective_id=0, has_side_effects=True, vmem_limit_bytes=50 * 1024 * 1024
        ),
        cost_estimate=pl.CostEstimate(
            flops=2 * length * width * (units + feats),
            bytes_accessed=2 * (length + width) * (units + feats),
            transcendentals=0,
        ),
        name="projected_grads",
    )(*(pltpu.with_memory_space_constraint(x, pltpu.HBM) for x in (hidden, grad_out, proj_in, proj_out)))
    height, wide = total_len // n_dp, total_len // n_tensor
    block = min(wide, 512)
    return pl.pallas_call(
        functools.partial(covariance_kernel, n_dp, n_tensor, total_len),
        out_shape=jax.ShapeDtypeStruct((height, wide), f32),
        in_specs=[vmem],
        out_specs=pl.BlockSpec(memory_space=pltpu.HBM),
        scratch_shapes=[dma((wide // block,)), pltpu.VMEM((wide // block, height, block), f32)],
        compiler_params=pltpu.CompilerParams(vmem_limit_bytes=16 * 1024 * 1024),
        name="covariance",
    )(gathered.reshape(n_dp * slot, LANES))


def solution(mesh):
    placed = (
        P("dp", None, "tensor"),
        P("dp", None, "tensor"),
        P(None, "tensor"),
        P(None, "tensor"),
    )
    return jax.shard_map(
        functools.partial(shards, mesh.shape["dp"], mesh.shape["tensor"]),
        mesh=mesh, in_specs=placed, out_specs=P("dp", "tensor"), check_vma=False,
    )
```

```python
import functools
import math

import jax
import jax.numpy as jnp
from jax import lax
from jax.experimental import pallas as pl
from jax.experimental.pallas import tpu as pltpu
from jax.sharding import PartitionSpec as P

MESH = pl.DeviceIdType.MESH
LANES = 128
AHEAD = 18


def chunk_of(size, largest=1024):
    best = size
    for part in range(LANES, largest + 1, LANES):
        if size % part == 0:
            best = part
    return best


def both_parts(x):
    high = x.astype(jnp.bfloat16)
    low = (x - high.astype(jnp.float32)).astype(jnp.bfloat16)
    return jnp.concatenate([high, low], axis=0)


def contract_last(a, b):
    return lax.dot_general(a, b, (((1,), (1,)), ((), ())), preferred_element_type=jnp.float32)


def grads_kernel(
    n_dp, n_tensor, inv_root,
    hidden, grad_out, proj_in, proj_out,
    gathered,
    h_buf, g_buf, wi_buf, wo_buf,
    in_panel, out_panel, out_others, part, flat, flat_others, message,
    h_sem, g_sem, wi_sem, wo_sem,
    panel_send, panel_recv, part_send, part_recv, message_send, message_recv,
):
    dp = lax.axis_index("dp")
    ts = lax.axis_index("tensor")
    h_chunks, _, h_wide = h_buf.shape
    g_chunks, _, g_wide = g_buf.shape
    flat_rows = flat.shape[0]
    own_rows = flat_rows // n_tensor
    row_rows = flat_rows // n_dp
    used = own_rows + row_rows + 1

    def h_copy(c):
        return pltpu.make_async_copy(
            hidden.at[0, :, pl.ds(pl.multiple_of(c * h_wide, LANES), h_wide)], h_buf.at[c], h_sem.at[c]
        )

    def g_copy(c):
        return pltpu.make_async_copy(
            grad_out.at[0, :, pl.ds(pl.multiple_of(c * g_wide, LANES), g_wide)], g_buf.at[c], g_sem.at[c]
        )

    def wi_copy(c):
        return pltpu.make_async_copy(
            proj_in.at[:, pl.ds(pl.multiple_of(c * h_wide, LANES), h_wide)], wi_buf.at[c], wi_sem.at[c]
        )

    def wo_copy(c):
        return pltpu.make_async_copy(
            proj_out.at[:, pl.ds(pl.multiple_of(c * g_wide, LANES), g_wide)], wo_buf.at[c], wo_sem.at[c]
        )

    copies = [(wo_copy, g_copy, c) for c in range(g_chunks)] + [(wi_copy, h_copy, c) for c in range(h_chunks)]

    def begin(k):
        if k < len(copies):
            weight, data, c = copies[k]
            weight(c).start()
            data(c).start()

    for k in range(AHEAD):
        begin(k)

    barrier = pltpu.get_barrier_semaphore()
    n_all = n_dp * n_tensor

    def greet(i, carry):
        other = lax.rem(dp * n_tensor + ts + i, n_all)
        pl.semaphore_signal(
            barrier, inc=1, device_id=(other // n_tensor, lax.rem(other, n_tensor)), device_id_type=MESH
        )
        return carry

    lax.fori_loop(1, n_all, greet, 0)

    for c in range(g_chunks):
        wo_copy(c).wait()
        g_copy(c).wait()
        begin(c + AHEAD)
        term = contract_last(wo_buf[c], g_buf[c])
        if c == 0:
            out_panel[...] = term
        else:
            out_panel[...] += term

    pl.semaphore_wait(barrier, n_all - 1)

    def panel_copy(i):
        return pltpu.make_async_remote_copy(
            src_ref=out_panel,
            dst_ref=out_others.at[i - 1],
            send_sem=panel_send.at[i - 1],
            recv_sem=panel_recv.at[i - 1],
            device_id=(dp, lax.rem(ts + i, n_tensor)),
            device_id_type=MESH,
        )

    for i in range(1, n_tensor):
        panel_copy(i).start()

    for c in range(h_chunks):
        wi_copy(c).wait()
        h_copy(c).wait()
        begin(g_chunks + c + AHEAD)
        term = contract_last(wi_buf[c], h_buf[c])
        if c == 0:
            in_panel[...] = term
        else:
            in_panel[...] += term

    for i in range(1, n_tensor):
        panel_copy(i).wait()

    total = out_panel[...]
    for i in range(1, n_tensor):
        total = total + out_others[i - 1]
    width = in_panel.shape[0]
    products = contract_last(both_parts(in_panel[...]), both_parts(total))
    sums = products[:width, :width] + products[:width, width:] + products[width:, :width]
    part[...] = sums * inv_root
    even = part[pl.ds(0, width // 2, 2), :]
    odd = part[pl.ds(1, width // 2, 2), :]
    flat[...] = jnp.concatenate([even, odd], axis=1)

    def part_copy(i):
        return pltpu.make_async_remote_copy(
            src_ref=flat,
            dst_ref=flat_others.at[i - 1],
            send_sem=part_send.at[i - 1],
            recv_sem=part_recv.at[i - 1],
            device_id=(dp, lax.rem(ts + i, n_tensor)),
            device_id_type=MESH,
        )

    for i in range(1, n_tensor):
        part_copy(i).start()
    for i in range(1, n_tensor):
        part_copy(i).wait()
    grads = flat[...]
    for i in range(1, n_tensor):
        grads = grads + flat_others[i - 1]
    mine = grads[:own_rows]
    for j in range(1, n_tensor):
        mine = jnp.where(ts == j, grads[j * own_rows:(j + 1) * own_rows], mine)
    square = jnp.broadcast_to(jnp.sum(grads * grads), (1, LANES))
    for d in range(n_dp):
        message[d, :own_rows] = mine
        message[d, own_rows:own_rows + row_rows] = grads[d * row_rows:(d + 1) * row_rows]
        message[d, own_rows + row_rows:used] = square

    def message_copy(i):
        to = lax.rem(dp + i, n_dp)
        return pltpu.make_async_remote_copy(
            src_ref=message.at[to, pl.ds(0, used)],
            dst_ref=gathered.at[i, pl.ds(0, used)],
            send_sem=message_send.at[i],
            recv_sem=message_recv.at[i],
            device_id=(to, ts),
            device_id_type=MESH,
        )

    for i in range(1, n_dp):
        message_copy(i).start()
    gathered[0] = message[dp]
    for i in range(1, n_dp):
        message_copy(i).wait()


def covariance_kernel(n_dp, n_tensor, total_len, gathered, out, block_sem, result):
    dp = lax.axis_index("dp")
    ts = lax.axis_index("tensor")
    height, wide = out.shape
    row_rows = height // LANES
    own_rows = wide // LANES
    slot = gathered.shape[0] // n_dp
    blocks, _, block = result.shape
    here = block // LANES

    def high_low(first, count):
        tiles = [gathered[pl.ds(first + k, n_dp, slot), :] for k in range(count)]
        x = jnp.concatenate(tiles, axis=1)
        high = x.astype(jnp.bfloat16).astype(jnp.float32)
        return high, x - high

    left_high, left_low = high_low(own_rows, row_rows)
    left = jnp.concatenate([left_high, left_low, left_high], axis=0) * (1.0 / n_dp)
    left = left.T.astype(jnp.bfloat16)
    squares = jnp.sum(gathered[pl.ds(own_rows + row_rows, n_dp, slot), :], axis=0, keepdims=True)
    damping = squares * (0.5 / (n_dp * total_len))
    diagonal = dp * height - ts * wide

    def block_copy(b):
        return pltpu.make_async_copy(result.at[b], out.at[:, pl.ds(b * block, block)], block_sem.at[b])

    for b in range(blocks):
        right_high, right_low = high_low(b * here, here)
        right = jnp.concatenate([right_high, right_high, right_low], axis=0).astype(jnp.bfloat16)
        result[b] = jnp.dot(left, right, preferred_element_type=jnp.float32)
        for k in range(block // height):
            @pl.when(diagonal == b * block + k * height)
            def _():
                for r in range(row_rows):
                    place = (pl.ds(r * LANES, LANES), pl.ds(k * height + r * LANES, LANES))
                    ids = lax.broadcasted_iota(jnp.int32, (LANES, LANES), 0)
                    same = ids == lax.broadcasted_iota(jnp.int32, (LANES, LANES), 1)
                    result[(b, *place)] += jnp.where(same, damping, jnp.float32(0.0))
        block_copy(b).start()
    for b in range(blocks):
        block_copy(b).wait()


def shards(n_dp, n_tensor, hidden, grad_out, proj_in, proj_out):
    seqs_here, length, units = hidden.shape
    assert seqs_here == 1
    feats = grad_out.shape[2]
    width = proj_in.shape[0]
    total_len = width * width
    flat_rows = total_len // LANES
    own_rows = flat_rows // n_tensor
    row_rows = flat_rows // n_dp
    slot = -(-(own_rows + row_rows + 1) // 8) * 8
    h_wide, g_wide = chunk_of(units), chunk_of(feats)
    h_chunks, g_chunks = units // h_wide, feats // g_wide
    peers = max(n_tensor - 1, 1)
    f32, bf16 = jnp.float32, jnp.bfloat16
    vmem = pl.BlockSpec(memory_space=pltpu.VMEM)
    in_hbm = pl.BlockSpec(memory_space=pltpu.HBM)
    dma = pltpu.SemaphoreType.DMA
    gathered = pl.pallas_call(
        functools.partial(grads_kernel, n_dp, n_tensor, 1.0 / math.sqrt(length)),
        out_shape=jax.ShapeDtypeStruct((n_dp, slot, LANES), f32),
        in_specs=[in_hbm] * 4,
        out_specs=vmem,
        scratch_shapes=[
            pltpu.VMEM((h_chunks, length, h_wide), bf16),
            pltpu.VMEM((g_chunks, length, g_wide), bf16),
            pltpu.VMEM((h_chunks, width, h_wide), bf16),
            pltpu.VMEM((g_chunks, width, g_wide), bf16),
            pltpu.VMEM((width, length), f32),
            pltpu.VMEM((width, length), f32),
            pltpu.VMEM((peers, width, length), f32),
            pltpu.VMEM((width, width), f32),
            pltpu.VMEM((flat_rows, LANES), f32),
            pltpu.VMEM((peers, flat_rows, LANES), f32),
            pltpu.VMEM((n_dp, slot, LANES), f32),
            dma((h_chunks,)),
            dma((g_chunks,)),
            dma((h_chunks,)),
            dma((g_chunks,)),
            dma((peers,)),
            dma((peers,)),
            dma((peers,)),
            dma((peers,)),
            dma((n_dp,)),
            dma((n_dp,)),
        ],
        compiler_params=pltpu.CompilerParams(
            collective_id=0, has_side_effects=True, vmem_limit_bytes=50 * 1024 * 1024
        ),
        cost_estimate=pl.CostEstimate(
            flops=2 * length * width * (units + feats),
            bytes_accessed=2 * (length + width) * (units + feats),
            transcendentals=0,
        ),
        name="projected_grads",
    )(*(pltpu.with_memory_space_constraint(x, pltpu.HBM) for x in (hidden, grad_out, proj_in, proj_out)))
    height, wide = total_len // n_dp, total_len // n_tensor
    block = min(wide, 512)
    return pl.pallas_call(
        functools.partial(covariance_kernel, n_dp, n_tensor, total_len),
        out_shape=jax.ShapeDtypeStruct((height, wide), f32),
        in_specs=[vmem],
        out_specs=pl.BlockSpec(memory_space=pltpu.HBM),
        scratch_shapes=[dma((wide // block,)), pltpu.VMEM((wide // block, height, block), f32)],
        compiler_params=pltpu.CompilerParams(vmem_limit_bytes=16 * 1024 * 1024),
        name="covariance",
    )(gathered.reshape(n_dp * slot, LANES))


def solution(mesh):
    placed = (
        P("dp", None, "tensor"),
        P("dp", None, "tensor"),
        P(None, "tensor"),
        P(None, "tensor"),
    )
    return jax.shard_map(
        functools.partial(shards, mesh.shape["dp"], mesh.shape["tensor"]),
        mesh=mesh, in_specs=placed, out_specs=P("dp", "tensor"), check_vma=False,
    )
```

```python
import functools
import math

import jax
import jax.numpy as jnp
from jax import lax
from jax.experimental import pallas as pl
from jax.experimental.pallas import tpu as pltpu
from jax.sharding import PartitionSpec as P

MESH = pl.DeviceIdType.MESH
LANES = 128
AHEAD = 3


def chunk_of(size, largest=1024):
    best = size
    for part in range(LANES, largest + 1, LANES):
        if size % part == 0:
            best = part
    return best


def groups_of(count, first, last):
    runs, c = [], 0
    while c < count:
        size = 1 if c < first or c >= count - last or c + 1 >= count - last else 2
        runs.append(list(range(c, c + size)))
        c += size
    return runs


def both_parts(x):
    high = x.astype(jnp.bfloat16)
    low = (x - high.astype(jnp.float32)).astype(jnp.bfloat16)
    return jnp.concatenate([high, low], axis=0)


def contract_last(a, b):
    return lax.dot_general(a, b, (((1,), (1,)), ((), ())), preferred_element_type=jnp.float32)


def grads_kernel(
    n_dp, n_tensor, inv_root,
    hidden, grad_out, proj_in, proj_out,
    gathered,
    h_buf, g_buf, wi_buf, wo_buf,
    in_panel, out_panel, out_others, total_parts, part, flat, flat_others, message,
    h_sem, g_sem, wi_sem, wo_sem,
    panel_send, panel_recv, part_send, part_recv, message_send, message_recv,
):
    dp = lax.axis_index("dp")
    ts = lax.axis_index("tensor")
    h_chunks, _, h_wide = h_buf.shape
    g_chunks, _, g_wide = g_buf.shape
    flat_rows = flat.shape[0]
    own_rows = flat_rows // n_tensor
    row_rows = flat_rows // n_dp
    used = own_rows + row_rows + 1

    def h_copy(c):
        return pltpu.make_async_copy(
            hidden.at[0, :, pl.ds(pl.multiple_of(c * h_wide, LANES), h_wide)], h_buf.at[c], h_sem.at[c]
        )

    def g_copy(c):
        return pltpu.make_async_copy(
            grad_out.at[0, :, pl.ds(pl.multiple_of(c * g_wide, LANES), g_wide)], g_buf.at[c], g_sem.at[c]
        )

    def wi_copy(c):
        return pltpu.make_async_copy(
            proj_in.at[:, pl.ds(pl.multiple_of(c * h_wide, LANES), h_wide)], wi_buf.at[c], wi_sem.at[c]
        )

    def wo_copy(c):
        return pltpu.make_async_copy(
            proj_out.at[:, pl.ds(pl.multiple_of(c * g_wide, LANES), g_wide)], wo_buf.at[c], wo_sem.at[c]
        )

    copies = [(wo_copy, g_copy, c) for c in range(g_chunks)] + [(wi_copy, h_copy, c) for c in range(h_chunks)]

    def begin(k):
        if k < len(copies):
            weight, data, c = copies[k]
            weight(c).start()
            data(c).start()

    for k in range(AHEAD):
        begin(k)

    barrier = pltpu.get_barrier_semaphore()
    n_all = n_dp * n_tensor

    def greet(i, carry):
        other = lax.rem(dp * n_tensor + ts + i, n_all)
        pl.semaphore_signal(
            barrier, inc=1, device_id=(other // n_tensor, lax.rem(other, n_tensor)), device_id_type=MESH
        )
        return carry

    lax.fori_loop(1, n_all, greet, 0)

    def project(group, weights, data, weight_copy, data_copy, before, panel):
        for c in group:
            weight_copy(c).wait()
            data_copy(c).wait()
            begin(before + c + AHEAD)
        term = contract_last(weights[group[0]], data[group[0]])
        for c in group[1:]:
            term = term + contract_last(weights[c], data[c])
        if group[0] == 0:
            panel[...] = term
        else:
            panel[...] += term

    for group in groups_of(g_chunks, 1, 0):
        project(group, wo_buf, g_buf, wo_copy, g_copy, 0, out_panel)

    pl.semaphore_wait(barrier, n_all - 1)

    def panel_copy(i):
        return pltpu.make_async_remote_copy(
            src_ref=out_panel,
            dst_ref=out_others.at[i - 1],
            send_sem=panel_send.at[i - 1],
            recv_sem=panel_recv.at[i - 1],
            device_id=(dp, lax.rem(ts + i, n_tensor)),
            device_id_type=MESH,
        )

    for i in range(1, n_tensor):
        panel_copy(i).start()

    in_groups = groups_of(h_chunks, 0, 2)
    for group in in_groups[:-1]:
        project(group, wi_buf, h_buf, wi_copy, h_copy, g_chunks, in_panel)
    for i in range(1, n_tensor):
        panel_copy(i).wait()
    total = out_panel[...]
    for i in range(1, n_tensor):
        total = total + out_others[i - 1]
    total_parts[...] = both_parts(total)
    project(in_groups[-1], wi_buf, h_buf, wi_copy, h_copy, g_chunks, in_panel)

    width = in_panel.shape[0]
    products = contract_last(both_parts(in_panel[...]), total_parts[...])
    sums = products[:width, :width] + products[:width, width:] + products[width:, :width]
    part[...] = sums * inv_root
    even = part[pl.ds(0, width // 2, 2), :]
    odd = part[pl.ds(1, width // 2, 2), :]
    flat[...] = jnp.concatenate([even, odd], axis=1)

    def part_copy(i):
        return pltpu.make_async_remote_copy(
            src_ref=flat,
            dst_ref=flat_others.at[i - 1],
            send_sem=part_send.at[i - 1],
            recv_sem=part_recv.at[i - 1],
            device_id=(dp, lax.rem(ts + i, n_tensor)),
            device_id_type=MESH,
        )

    for i in range(1, n_tensor):
        part_copy(i).start()
    for i in range(1, n_tensor):
        part_copy(i).wait()
    grads = flat[...]
    for i in range(1, n_tensor):
        grads = grads + flat_others[i - 1]
    mine = grads[:own_rows]
    for j in range(1, n_tensor):
        mine = jnp.where(ts == j, grads[j * own_rows:(j + 1) * own_rows], mine)
    square = jnp.broadcast_to(jnp.sum(grads * grads), (1, LANES))
    for d in range(n_dp):
        message[d, :own_rows] = mine
        message[d, own_rows:own_rows + row_rows] = grads[d * row_rows:(d + 1) * row_rows]
        message[d, own_rows + row_rows:used] = square

    def message_copy(i):
        to = lax.rem(dp + i, n_dp)
        return pltpu.make_async_remote_copy(
            src_ref=message.at[to, pl.ds(0, used)],
            dst_ref=gathered.at[i, pl.ds(0, used)],
            send_sem=message_send.at[i],
            recv_sem=message_recv.at[i],
            device_id=(to, ts),
            device_id_type=MESH,
        )

    for i in sorted(range(1, n_dp), key=lambda i: -min(i, n_dp - i)):
        message_copy(i).start()
    gathered[0] = message[dp]
    for i in range(1, n_dp):
        message_copy(i).wait()


def covariance_kernel(n_dp, n_tensor, total_len, gathered, out, block_sem, result):
    dp = lax.axis_index("dp")
    ts = lax.axis_index("tensor")
    height, wide = out.shape
    row_rows = height // LANES
    own_rows = wide // LANES
    slot = gathered.shape[0] // n_dp
    blocks, _, block = result.shape
    here = block // LANES

    def high_low(first, count):
        tiles = [gathered[pl.ds(first + k, n_dp, slot), :] for k in range(count)]
        x = jnp.concatenate(tiles, axis=1)
        high = x.astype(jnp.bfloat16).astype(jnp.float32)
        return high, x - high

    left_high, left_low = high_low(own_rows, row_rows)
    left = jnp.concatenate([left_high, left_low, left_high], axis=0) * (1.0 / n_dp)
    left = left.T.astype(jnp.bfloat16)
    squares = jnp.sum(gathered[pl.ds(own_rows + row_rows, n_dp, slot), :], axis=0, keepdims=True)
    damping = squares * (0.5 / (n_dp * total_len))
    diagonal = dp * height - ts * wide

    def block_copy(b):
        return pltpu.make_async_copy(result.at[b], out.at[:, pl.ds(b * block, block)], block_sem.at[b])

    for b in range(blocks):
        right_high, right_low = high_low(b * here, here)
        right = jnp.concatenate([right_high, right_high, right_low], axis=0).astype(jnp.bfloat16)
        result[b] = jnp.dot(left, right, preferred_element_type=jnp.float32)
        for k in range(block // height):
            @pl.when(diagonal == b * block + k * height)
            def _():
                for r in range(row_rows):
                    place = (pl.ds(r * LANES, LANES), pl.ds(k * height + r * LANES, LANES))
                    ids = lax.broadcasted_iota(jnp.int32, (LANES, LANES), 0)
                    same = ids == lax.broadcasted_iota(jnp.int32, (LANES, LANES), 1)
                    result[(b, *place)] += jnp.where(same, damping, jnp.float32(0.0))
        block_copy(b).start()
    for b in range(blocks):
        block_copy(b).wait()


def shards(n_dp, n_tensor, hidden, grad_out, proj_in, proj_out):
    seqs_here, length, units = hidden.shape
    assert seqs_here == 1
    feats = grad_out.shape[2]
    width = proj_in.shape[0]
    total_len = width * width
    flat_rows = total_len // LANES
    own_rows = flat_rows // n_tensor
    row_rows = flat_rows // n_dp
    slot = -(-(own_rows + row_rows + 1) // 8) * 8
    h_wide, g_wide = chunk_of(units), chunk_of(feats)
    h_chunks, g_chunks = units // h_wide, feats // g_wide
    peers = max(n_tensor - 1, 1)
    f32, bf16 = jnp.float32, jnp.bfloat16
    vmem = pl.BlockSpec(memory_space=pltpu.VMEM)
    in_hbm = pl.BlockSpec(memory_space=pltpu.HBM)
    dma = pltpu.SemaphoreType.DMA
    gathered = pl.pallas_call(
        functools.partial(grads_kernel, n_dp, n_tensor, 1.0 / math.sqrt(length)),
        out_shape=jax.ShapeDtypeStruct((n_dp, slot, LANES), f32),
        in_specs=[in_hbm] * 4,
        out_specs=vmem,
        scratch_shapes=[
            pltpu.VMEM((h_chunks, length, h_wide), bf16),
            pltpu.VMEM((g_chunks, length, g_wide), bf16),
            pltpu.VMEM((h_chunks, width, h_wide), bf16),
            pltpu.VMEM((g_chunks, width, g_wide), bf16),
            pltpu.VMEM((width, length), f32),
            pltpu.VMEM((width, length), f32),
            pltpu.VMEM((peers, width, length), f32),
            pltpu.VMEM((2 * width, length), bf16),
            pltpu.VMEM((width, width), f32),
            pltpu.VMEM((flat_rows, LANES), f32),
            pltpu.VMEM((peers, flat_rows, LANES), f32),
            pltpu.VMEM((n_dp, slot, LANES), f32),
            dma((h_chunks,)),
            dma((g_chunks,)),
            dma((h_chunks,)),
            dma((g_chunks,)),
            dma((peers,)),
            dma((peers,)),
            dma((peers,)),
            dma((peers,)),
            dma((n_dp,)),
            dma((n_dp,)),
        ],
        compiler_params=pltpu.CompilerParams(
            collective_id=0, has_side_effects=True, vmem_limit_bytes=50 * 1024 * 1024
        ),
        cost_estimate=pl.CostEstimate(
            flops=2 * length * width * (units + feats),
            bytes_accessed=2 * (length + width) * (units + feats),
            transcendentals=0,
        ),
        name="projected_grads",
    )(*(pltpu.with_memory_space_constraint(x, pltpu.HBM) for x in (hidden, grad_out, proj_in, proj_out)))
    height, wide = total_len // n_dp, total_len // n_tensor
    block = min(wide, 512)
    return pl.pallas_call(
        functools.partial(covariance_kernel, n_dp, n_tensor, total_len),
        out_shape=jax.ShapeDtypeStruct((height, wide), f32),
        in_specs=[vmem],
        out_specs=pl.BlockSpec(memory_space=pltpu.HBM),
        scratch_shapes=[dma((wide // block,)), pltpu.VMEM((wide // block, height, block), f32)],
        compiler_params=pltpu.CompilerParams(vmem_limit_bytes=16 * 1024 * 1024),
        name="covariance",
    )(gathered.reshape(n_dp * slot, LANES))


def solution(mesh):
    placed = (
        P("dp", None, "tensor"),
        P("dp", None, "tensor"),
        P(None, "tensor"),
        P(None, "tensor"),
    )
    return jax.shard_map(
        functools.partial(shards, mesh.shape["dp"], mesh.shape["tensor"]),
        mesh=mesh, in_specs=placed, out_specs=P("dp", "tensor"), check_vma=False,
    )
```

```python
import functools
import math

import jax
import jax.numpy as jnp
from jax import lax
from jax.experimental import pallas as pl
from jax.experimental.pallas import tpu as pltpu
from jax.sharding import PartitionSpec as P

MESH = pl.DeviceIdType.MESH
LANES = 128
AHEAD = 12


def chunk_of(size, largest=512):
    best = size
    for part in range(LANES, largest + 1, LANES):
        if size % part == 0:
            best = part
    return best


def groups_of(count, first, last):
    runs, c = [], 0
    while c < count:
        size = 1 if c < first or c >= count - last or c + 1 >= count - last else 2
        runs.append(list(range(c, c + size)))
        c += size
    return runs


def both_parts(x):
    high = x.astype(jnp.bfloat16)
    low = (x - high.astype(jnp.float32)).astype(jnp.bfloat16)
    return jnp.concatenate([high, low], axis=0)


def contract_last(a, b):
    return lax.dot_general(a, b, (((1,), (1,)), ((), ())), preferred_element_type=jnp.float32)


def grads_kernel(
    n_dp, n_tensor, inv_root,
    hidden, grad_out, proj_in, proj_out,
    gathered,
    h_buf, g_buf, wi_buf, wo_buf,
    in_panel, out_panel, out_others, total_parts, part, flat, flat_others, message,
    h_sem, g_sem, wi_sem, wo_sem,
    panel_send, panel_recv, part_send, part_recv, message_send, message_recv,
):
    dp = lax.axis_index("dp")
    ts = lax.axis_index("tensor")
    h_chunks, _, h_wide = h_buf.shape
    g_chunks, _, g_wide = g_buf.shape
    flat_rows = flat.shape[0]
    own_rows = flat_rows // n_tensor
    row_rows = flat_rows // n_dp
    used = own_rows + row_rows + 1

    def h_copy(c):
        return pltpu.make_async_copy(
            hidden.at[0, :, pl.ds(pl.multiple_of(c * h_wide, LANES), h_wide)], h_buf.at[c], h_sem.at[c]
        )

    def g_copy(c):
        return pltpu.make_async_copy(
            grad_out.at[0, :, pl.ds(pl.multiple_of(c * g_wide, LANES), g_wide)], g_buf.at[c], g_sem.at[c]
        )

    def wi_copy(c):
        return pltpu.make_async_copy(
            proj_in.at[:, pl.ds(pl.multiple_of(c * h_wide, LANES), h_wide)], wi_buf.at[c], wi_sem.at[c]
        )

    def wo_copy(c):
        return pltpu.make_async_copy(
            proj_out.at[:, pl.ds(pl.multiple_of(c * g_wide, LANES), g_wide)], wo_buf.at[c], wo_sem.at[c]
        )

    copies = [(wo_copy, g_copy, c) for c in range(g_chunks)] + [(wi_copy, h_copy, c) for c in range(h_chunks)]

    def begin(k):
        if k < len(copies):
            weight, data, c = copies[k]
            weight(c).start()
            data(c).start()

    for k in range(AHEAD):
        begin(k)

    barrier = pltpu.get_barrier_semaphore()
    n_all = n_dp * n_tensor

    def greet(i, carry):
        other = lax.rem(dp * n_tensor + ts + i, n_all)
        pl.semaphore_signal(
            barrier, inc=1, device_id=(other // n_tensor, lax.rem(other, n_tensor)), device_id_type=MESH
        )
        return carry

    lax.fori_loop(1, n_all, greet, 0)

    def project(group, weights, data, weight_copy, data_copy, before, panel):
        for c in group:
            weight_copy(c).wait()
            data_copy(c).wait()
            begin(before + c + AHEAD)
        term = contract_last(weights[group[0]], data[group[0]])
        for c in group[1:]:
            term = term + contract_last(weights[c], data[c])
        if group[0] == 0:
            panel[...] = term
        else:
            panel[...] += term

    for group in groups_of(g_chunks, 1, 0):
        project(group, wo_buf, g_buf, wo_copy, g_copy, 0, out_panel)

    pl.semaphore_wait(barrier, n_all - 1)

    def panel_copy(i):
        return pltpu.make_async_remote_copy(
            src_ref=out_panel,
            dst_ref=out_others.at[i - 1],
            send_sem=panel_send.at[i - 1],
            recv_sem=panel_recv.at[i - 1],
            device_id=(dp, lax.rem(ts + i, n_tensor)),
            device_id_type=MESH,
        )

    for i in range(1, n_tensor):
        panel_copy(i).start()

    in_groups = groups_of(h_chunks, 0, 2)
    for group in in_groups[:-1]:
        project(group, wi_buf, h_buf, wi_copy, h_copy, g_chunks, in_panel)
    for i in range(1, n_tensor):
        panel_copy(i).wait()
    total = out_panel[...]
    for i in range(1, n_tensor):
        total = total + out_others[i - 1]
    total_parts[...] = both_parts(total)
    project(in_groups[-1], wi_buf, h_buf, wi_copy, h_copy, g_chunks, in_panel)

    width = in_panel.shape[0]
    products = contract_last(both_parts(in_panel[...]), total_parts[...])
    sums = products[:width, :width] + products[:width, width:] + products[width:, :width]
    part[...] = sums * inv_root
    even = part[pl.ds(0, width // 2, 2), :]
    odd = part[pl.ds(1, width // 2, 2), :]
    flat[...] = jnp.concatenate([even, odd], axis=1)

    def part_copy(i):
        return pltpu.make_async_remote_copy(
            src_ref=flat,
            dst_ref=flat_others.at[i - 1],
            send_sem=part_send.at[i - 1],
            recv_sem=part_recv.at[i - 1],
            device_id=(dp, lax.rem(ts + i, n_tensor)),
            device_id_type=MESH,
        )

    for i in range(1, n_tensor):
        part_copy(i).start()
    for i in range(1, n_tensor):
        part_copy(i).wait()
    grads = flat[...]
    for i in range(1, n_tensor):
        grads = grads + flat_others[i - 1]
    mine = grads[:own_rows]
    for j in range(1, n_tensor):
        mine = jnp.where(ts == j, grads[j * own_rows:(j + 1) * own_rows], mine)
    square = jnp.broadcast_to(jnp.sum(grads * grads), (1, LANES))
    for d in range(n_dp):
        message[d, :own_rows] = mine
        message[d, own_rows:own_rows + row_rows] = grads[d * row_rows:(d + 1) * row_rows]
        message[d, own_rows + row_rows:used] = square

    def message_copy(i):
        to = lax.rem(dp + i, n_dp)
        return pltpu.make_async_remote_copy(
            src_ref=message.at[to, pl.ds(0, used)],
            dst_ref=gathered.at[i, pl.ds(0, used)],
            send_sem=message_send.at[i],
            recv_sem=message_recv.at[i],
            device_id=(to, ts),
            device_id_type=MESH,
        )

    for i in sorted(range(1, n_dp), key=lambda i: -min(i, n_dp - i)):
        message_copy(i).start()
    gathered[0] = message[dp]
    for i in range(1, n_dp):
        message_copy(i).wait()


def covariance_kernel(n_dp, n_tensor, total_len, gathered, out, block_sem, result):
    dp = lax.axis_index("dp")
    ts = lax.axis_index("tensor")
    height, wide = out.shape
    row_rows = height // LANES
    own_rows = wide // LANES
    slot = gathered.shape[0] // n_dp
    blocks, _, block = result.shape
    here = block // LANES

    def high_low(first, count):
        tiles = [gathered[pl.ds(first + k, n_dp, slot), :] for k in range(count)]
        x = jnp.concatenate(tiles, axis=1)
        high = x.astype(jnp.bfloat16).astype(jnp.float32)
        return high, x - high

    left_high, left_low = high_low(own_rows, row_rows)
    left = jnp.concatenate([left_high, left_low, left_high], axis=0) * (1.0 / n_dp)
    left = left.T.astype(jnp.bfloat16)
    squares = jnp.sum(gathered[pl.ds(own_rows + row_rows, n_dp, slot), :], axis=0, keepdims=True)
    damping = squares * (0.5 / (n_dp * total_len))
    diagonal = dp * height - ts * wide

    def block_copy(b):
        return pltpu.make_async_copy(result.at[b], out.at[:, pl.ds(b * block, block)], block_sem.at[b])

    for b in range(blocks):
        right_high, right_low = high_low(b * here, here)
        right = jnp.concatenate([right_high, right_high, right_low], axis=0).astype(jnp.bfloat16)
        result[b] = jnp.dot(left, right, preferred_element_type=jnp.float32)
        for k in range(block // height):
            @pl.when(diagonal == b * block + k * height)
            def _():
                for r in range(row_rows):
                    place = (pl.ds(r * LANES, LANES), pl.ds(k * height + r * LANES, LANES))
                    ids = lax.broadcasted_iota(jnp.int32, (LANES, LANES), 0)
                    same = ids == lax.broadcasted_iota(jnp.int32, (LANES, LANES), 1)
                    result[(b, *place)] += jnp.where(same, damping, jnp.float32(0.0))
        block_copy(b).start()
    for b in range(blocks):
        block_copy(b).wait()


def shards(n_dp, n_tensor, hidden, grad_out, proj_in, proj_out):
    seqs_here, length, units = hidden.shape
    assert seqs_here == 1
    feats = grad_out.shape[2]
    width = proj_in.shape[0]
    total_len = width * width
    flat_rows = total_len // LANES
    own_rows = flat_rows // n_tensor
    row_rows = flat_rows // n_dp
    slot = -(-(own_rows + row_rows + 1) // 8) * 8
    h_wide, g_wide = chunk_of(units), chunk_of(feats)
    h_chunks, g_chunks = units // h_wide, feats // g_wide
    peers = max(n_tensor - 1, 1)
    f32, bf16 = jnp.float32, jnp.bfloat16
    vmem = pl.BlockSpec(memory_space=pltpu.VMEM)
    in_hbm = pl.BlockSpec(memory_space=pltpu.HBM)
    dma = pltpu.SemaphoreType.DMA
    gathered = pl.pallas_call(
        functools.partial(grads_kernel, n_dp, n_tensor, 1.0 / math.sqrt(length)),
        out_shape=jax.ShapeDtypeStruct((n_dp, slot, LANES), f32),
        in_specs=[in_hbm] * 4,
        out_specs=vmem,
        scratch_shapes=[
            pltpu.VMEM((h_chunks, length, h_wide), bf16),
            pltpu.VMEM((g_chunks, length, g_wide), bf16),
            pltpu.VMEM((h_chunks, width, h_wide), bf16),
            pltpu.VMEM((g_chunks, width, g_wide), bf16),
            pltpu.VMEM((width, length), f32),
            pltpu.VMEM((width, length), f32),
            pltpu.VMEM((peers, width, length), f32),
            pltpu.VMEM((2 * width, length), bf16),
            pltpu.VMEM((width, width), f32),
            pltpu.VMEM((flat_rows, LANES), f32),
            pltpu.VMEM((peers, flat_rows, LANES), f32),
            pltpu.VMEM((n_dp, slot, LANES), f32),
            dma((h_chunks,)),
            dma((g_chunks,)),
            dma((h_chunks,)),
            dma((g_chunks,)),
            dma((peers,)),
            dma((peers,)),
            dma((peers,)),
            dma((peers,)),
            dma((n_dp,)),
            dma((n_dp,)),
        ],
        compiler_params=pltpu.CompilerParams(
            collective_id=0, has_side_effects=True, vmem_limit_bytes=50 * 1024 * 1024
        ),
        cost_estimate=pl.CostEstimate(
            flops=2 * length * width * (units + feats),
            bytes_accessed=2 * (length + width) * (units + feats),
            transcendentals=0,
        ),
        name="projected_grads",
    )(*(pltpu.with_memory_space_constraint(x, pltpu.HBM) for x in (hidden, grad_out, proj_in, proj_out)))
    height, wide = total_len // n_dp, total_len // n_tensor
    block = min(wide, max(height, 256))
    return pl.pallas_call(
        functools.partial(covariance_kernel, n_dp, n_tensor, total_len),
        out_shape=jax.ShapeDtypeStruct((height, wide), f32),
        in_specs=[vmem],
        out_specs=pl.BlockSpec(memory_space=pltpu.HBM),
        scratch_shapes=[dma((wide // block,)), pltpu.VMEM((wide // block, height, block), f32)],
        compiler_params=pltpu.CompilerParams(vmem_limit_bytes=16 * 1024 * 1024),
        name="covariance",
    )(gathered.reshape(n_dp * slot, LANES))


def solution(mesh):
    placed = (
        P("dp", None, "tensor"),
        P("dp", None, "tensor"),
        P(None, "tensor"),
        P(None, "tensor"),
    )
    return jax.shard_map(
        functools.partial(shards, mesh.shape["dp"], mesh.shape["tensor"]),
        mesh=mesh, in_specs=placed, out_specs=P("dp", "tensor"), check_vma=False,
    )
```

```python
import functools
import math

import jax
import jax.numpy as jnp
from jax import lax
from jax.experimental import pallas as pl
from jax.experimental.pallas import tpu as pltpu
from jax.sharding import PartitionSpec as P

MESH = pl.DeviceIdType.MESH
LANES = 128
AHEAD = 6


def chunk_of(size, largest=1024):
    best = size
    for part in range(LANES, largest + 1, LANES):
        if size % part == 0:
            best = part
    return best


def groups_of(count, first, last):
    runs, c = [], 0
    while c < count:
        size = 1 if c < first or c >= count - last or c + 1 >= count - last else 2
        runs.append(list(range(c, c + size)))
        c += size
    return runs


def both_parts(x):
    high = x.astype(jnp.bfloat16)
    low = (x - high.astype(jnp.float32)).astype(jnp.bfloat16)
    return jnp.concatenate([high, low], axis=0)


def contract_last(a, b):
    return lax.dot_general(a, b, (((1,), (1,)), ((), ())), preferred_element_type=jnp.float32)


def grads_kernel(
    n_dp, n_tensor, inv_root,
    hidden, grad_out, proj_in, proj_out,
    gathered,
    h_buf, g_buf, wi_buf, wo_buf,
    in_panel, out_panel, out_others, total_parts, part, flat, flat_others, message,
    h_sem, g_sem, wi_sem, wo_sem,
    panel_send, panel_recv, part_send, part_recv, message_send, message_recv,
):
    dp = lax.axis_index("dp")
    ts = lax.axis_index("tensor")
    h_chunks, _, h_wide = h_buf.shape
    g_chunks, _, g_wide = g_buf.shape
    flat_rows = flat.shape[0]
    own_rows = flat_rows // n_tensor
    row_rows = flat_rows // n_dp
    used = own_rows + row_rows + 1

    def h_copy(c):
        return pltpu.make_async_copy(
            hidden.at[0, :, pl.ds(pl.multiple_of(c * h_wide, LANES), h_wide)], h_buf.at[c], h_sem.at[c]
        )

    def g_copy(c):
        return pltpu.make_async_copy(
            grad_out.at[0, :, pl.ds(pl.multiple_of(c * g_wide, LANES), g_wide)], g_buf.at[c], g_sem.at[c]
        )

    def wi_copy(c):
        return pltpu.make_async_copy(
            proj_in.at[:, pl.ds(pl.multiple_of(c * h_wide, LANES), h_wide)], wi_buf.at[c], wi_sem.at[c]
        )

    def wo_copy(c):
        return pltpu.make_async_copy(
            proj_out.at[:, pl.ds(pl.multiple_of(c * g_wide, LANES), g_wide)], wo_buf.at[c], wo_sem.at[c]
        )

    copies = [(wo_copy, g_copy, c) for c in range(g_chunks)] + [(wi_copy, h_copy, c) for c in range(h_chunks)]

    def begin(k):
        if k < len(copies):
            weight, data, c = copies[k]
            weight(c).start()
            data(c).start()

    for k in range(AHEAD):
        begin(k)

    barrier = pltpu.get_barrier_semaphore()
    n_all = n_dp * n_tensor

    def greet(i, carry):
        other = lax.rem(dp * n_tensor + ts + i, n_all)
        pl.semaphore_signal(
            barrier, inc=1, device_id=(other // n_tensor, lax.rem(other, n_tensor)), device_id_type=MESH
        )
        return carry

    lax.fori_loop(1, n_all, greet, 0)

    def project(group, weights, data, weight_copy, data_copy, before, panel):
        for c in group:
            weight_copy(c).wait()
            data_copy(c).wait()
            begin(before + c + AHEAD)
        term = contract_last(weights[group[0]], data[group[0]])
        for c in group[1:]:
            term = term + contract_last(weights[c], data[c])
        if group[0] == 0:
            panel[...] = term
        else:
            panel[...] += term

    for group in groups_of(g_chunks, 1, 0):
        project(group, wo_buf, g_buf, wo_copy, g_copy, 0, out_panel)

    pl.semaphore_wait(barrier, n_all - 1)

    def panel_copy(i):
        return pltpu.make_async_remote_copy(
            src_ref=out_panel,
            dst_ref=out_others.at[i - 1],
            send_sem=panel_send.at[i - 1],
            recv_sem=panel_recv.at[i - 1],
            device_id=(dp, lax.rem(ts + i, n_tensor)),
            device_id_type=MESH,
        )

    for i in range(1, n_tensor):
        panel_copy(i).start()

    in_groups = groups_of(h_chunks, 0, 2)
    for group in in_groups[:-1]:
        project(group, wi_buf, h_buf, wi_copy, h_copy, g_chunks, in_panel)
    for i in range(1, n_tensor):
        panel_copy(i).wait()
    total = out_panel[...]
    for i in range(1, n_tensor):
        total = total + out_others[i - 1]
    total_parts[...] = both_parts(total)
    project(in_groups[-1], wi_buf, h_buf, wi_copy, h_copy, g_chunks, in_panel)

    width = in_panel.shape[0]
    products = contract_last(both_parts(in_panel[...]), total_parts[...])
    sums = products[:width, :width] + products[:width, width:] + products[width:, :width]
    part[...] = sums * inv_root
    even = part[pl.ds(0, width // 2, 2), :]
    odd = part[pl.ds(1, width // 2, 2), :]
    flat[...] = jnp.concatenate([even, odd], axis=1)

    def part_copy(i):
        return pltpu.make_async_remote_copy(
            src_ref=flat,
            dst_ref=flat_others.at[i - 1],
            send_sem=part_send.at[i - 1],
            recv_sem=part_recv.at[i - 1],
            device_id=(dp, lax.rem(ts + i, n_tensor)),
            device_id_type=MESH,
        )

    for i in range(1, n_tensor):
        part_copy(i).start()
    for i in range(1, n_tensor):
        part_copy(i).wait()
    grads = flat[...]
    for i in range(1, n_tensor):
        grads = grads + flat_others[i - 1]
    mine = grads[:own_rows]
    for j in range(1, n_tensor):
        mine = jnp.where(ts == j, grads[j * own_rows:(j + 1) * own_rows], mine)
    square = jnp.broadcast_to(jnp.sum(grads * grads), (1, LANES))
    for d in range(n_dp):
        message[d, :own_rows] = mine
        message[d, own_rows:own_rows + row_rows] = grads[d * row_rows:(d + 1) * row_rows]
        message[d, own_rows + row_rows:used] = square

    def message_copy(k):
        to = k + (k >= dp).astype(jnp.int32)
        slot = lax.rem(to - dp + n_dp, n_dp)
        return pltpu.make_async_remote_copy(
            src_ref=message.at[to, pl.ds(0, used)],
            dst_ref=gathered.at[slot, pl.ds(0, used)],
            send_sem=message_send.at[k],
            recv_sem=message_recv.at[slot],
            device_id=(to, ts),
            device_id_type=MESH,
        )

    for k in range(n_dp - 1):
        message_copy(k).start()
    gathered[0] = message[dp]
    for i in range(1, n_dp):
        arrived = gathered.at[i, pl.ds(0, used)]
        pltpu.make_async_copy(arrived, arrived, message_recv.at[i]).wait()
    for k in range(n_dp - 1):
        message_copy(k).wait_send()


def covariance_kernel(n_dp, n_tensor, total_len, gathered, out, block_sem, result):
    dp = lax.axis_index("dp")
    ts = lax.axis_index("tensor")
    height, wide = out.shape
    row_rows = height // LANES
    own_rows = wide // LANES
    slot = gathered.shape[0] // n_dp
    blocks, _, block = result.shape
    here = block // LANES

    def high_low(first, count):
        tiles = [gathered[pl.ds(first + k, n_dp, slot), :] for k in range(count)]
        x = jnp.concatenate(tiles, axis=1)
        high = x.astype(jnp.bfloat16).astype(jnp.float32)
        return high, x - high

    left_high, left_low = high_low(own_rows, row_rows)
    left = jnp.concatenate([left_high, left_low, left_high], axis=0) * (1.0 / n_dp)
    left = left.T.astype(jnp.bfloat16)
    squares = jnp.sum(gathered[pl.ds(own_rows + row_rows, n_dp, slot), :], axis=0, keepdims=True)
    damping = squares * (0.5 / (n_dp * total_len))
    diagonal = dp * height - ts * wide

    def block_copy(b):
        return pltpu.make_async_copy(result.at[b], out.at[:, pl.ds(b * block, block)], block_sem.at[b])

    for b in range(blocks):
        right_high, right_low = high_low(b * here, here)
        right = jnp.concatenate([right_high, right_high, right_low], axis=0).astype(jnp.bfloat16)
        result[b] = jnp.dot(left, right, preferred_element_type=jnp.float32)
        @pl.when(jnp.logical_and(diagonal >= b * block, diagonal < (b + 1) * block))
        def _():
            for r in range(row_rows):
                first = pl.multiple_of(diagonal - b * block + r * LANES, LANES)
                place = (pl.ds(r * LANES, LANES), pl.ds(first, LANES))
                ids = lax.broadcasted_iota(jnp.int32, (LANES, LANES), 0)
                same = ids == lax.broadcasted_iota(jnp.int32, (LANES, LANES), 1)
                result[(b, *place)] += jnp.where(same, damping, jnp.float32(0.0))

        block_copy(b).start()
    for b in range(blocks):
        block_copy(b).wait()


def shards(n_dp, n_tensor, hidden, grad_out, proj_in, proj_out):
    seqs_here, length, units = hidden.shape
    assert seqs_here == 1
    feats = grad_out.shape[2]
    width = proj_in.shape[0]
    total_len = width * width
    flat_rows = total_len // LANES
    own_rows = flat_rows // n_tensor
    row_rows = flat_rows // n_dp
    slot = -(-(own_rows + row_rows + 1) // 8) * 8
    h_wide, g_wide = chunk_of(units), chunk_of(feats)
    h_chunks, g_chunks = units // h_wide, feats // g_wide
    peers = max(n_tensor - 1, 1)
    f32, bf16 = jnp.float32, jnp.bfloat16
    vmem = pl.BlockSpec(memory_space=pltpu.VMEM)
    in_hbm = pl.BlockSpec(memory_space=pltpu.HBM)
    dma = pltpu.SemaphoreType.DMA
    gathered = pl.pallas_call(
        functools.partial(grads_kernel, n_dp, n_tensor, 1.0 / math.sqrt(length)),
        out_shape=jax.ShapeDtypeStruct((n_dp, slot, LANES), f32),
        in_specs=[in_hbm] * 4,
        out_specs=vmem,
        scratch_shapes=[
            pltpu.VMEM((h_chunks, length, h_wide), bf16),
            pltpu.VMEM((g_chunks, length, g_wide), bf16),
            pltpu.VMEM((h_chunks, width, h_wide), bf16),
            pltpu.VMEM((g_chunks, width, g_wide), bf16),
            pltpu.VMEM((width, length), f32),
            pltpu.VMEM((width, length), f32),
            pltpu.VMEM((peers, width, length), f32),
            pltpu.VMEM((2 * width, length), bf16),
            pltpu.VMEM((width, width), f32),
            pltpu.VMEM((flat_rows, LANES), f32),
            pltpu.VMEM((peers, flat_rows, LANES), f32),
            pltpu.VMEM((n_dp, slot, LANES), f32),
            dma((h_chunks,)),
            dma((g_chunks,)),
            dma((h_chunks,)),
            dma((g_chunks,)),
            dma((peers,)),
            dma((peers,)),
            dma((peers,)),
            dma((peers,)),
            dma((n_dp,)),
            dma((n_dp,)),
        ],
        compiler_params=pltpu.CompilerParams(
            collective_id=0, has_side_effects=True, vmem_limit_bytes=50 * 1024 * 1024
        ),
        cost_estimate=pl.CostEstimate(
            flops=2 * length * width * (units + feats),
            bytes_accessed=2 * (length + width) * (units + feats),
            transcendentals=0,
        ),
        name="projected_grads",
    )(*(pltpu.with_memory_space_constraint(x, pltpu.HBM) for x in (hidden, grad_out, proj_in, proj_out)))
    height, wide = total_len // n_dp, total_len // n_tensor
    block = min(wide, 1024)
    return pl.pallas_call(
        functools.partial(covariance_kernel, n_dp, n_tensor, total_len),
        out_shape=jax.ShapeDtypeStruct((height, wide), f32),
        in_specs=[vmem],
        out_specs=pl.BlockSpec(memory_space=pltpu.HBM),
        scratch_shapes=[dma((wide // block,)), pltpu.VMEM((wide // block, height, block), f32)],
        compiler_params=pltpu.CompilerParams(vmem_limit_bytes=16 * 1024 * 1024),
        name="covariance",
    )(gathered.reshape(n_dp * slot, LANES))


def solution(mesh):
    placed = (
        P("dp", None, "tensor"),
        P("dp", None, "tensor"),
        P(None, "tensor"),
        P(None, "tensor"),
    )
    return jax.shard_map(
        functools.partial(shards, mesh.shape["dp"], mesh.shape["tensor"]),
        mesh=mesh, in_specs=placed, out_specs=P("dp", "tensor"), check_vma=False,
    )
```

```python
import functools
import math

import jax
import jax.numpy as jnp
from jax import lax
from jax.experimental import pallas as pl
from jax.experimental.pallas import tpu as pltpu
from jax.sharding import PartitionSpec as P

MESH = pl.DeviceIdType.MESH
LANES = 128
AHEAD = 6
FIRST = 2


def chunk_of(size, largest=1024):
    best = size
    for part in range(LANES, largest + 1, LANES):
        if size % part == 0:
            best = part
    return best


def groups_of(count, first, last):
    runs, c = [], 0
    while c < count:
        size = 1 if c < first or c >= count - last or c + 1 >= count - last else 2
        runs.append(list(range(c, c + size)))
        c += size
    return runs


def both_parts(x):
    high = x.astype(jnp.bfloat16)
    low = (x - high.astype(jnp.float32)).astype(jnp.bfloat16)
    return jnp.concatenate([high, low], axis=0)


def contract_last(a, b):
    return lax.dot_general(a, b, (((1,), (1,)), ((), ())), preferred_element_type=jnp.float32)


def grads_kernel(
    n_dp, n_tensor, inv_root,
    hidden, grad_out, proj_in, proj_out,
    gathered,
    h_buf, g_buf, wi_buf, wo_buf,
    in_panel, out_panel, out_others, total_parts, part, flat, flat_others, message,
    h_sem, g_sem, wi_sem, wo_sem,
    panel_send, panel_recv, part_send, part_recv, message_send, message_recv,
):
    dp = lax.axis_index("dp")
    ts = lax.axis_index("tensor")
    h_chunks, _, h_wide = h_buf.shape
    g_chunks, _, g_wide = g_buf.shape
    flat_rows = flat.shape[0]
    own_rows = flat_rows // n_tensor
    row_rows = flat_rows // n_dp
    used = own_rows + row_rows + 1

    def h_copy(c):
        return pltpu.make_async_copy(
            hidden.at[0, :, pl.ds(pl.multiple_of(c * h_wide, LANES), h_wide)], h_buf.at[c], h_sem.at[c]
        )

    def g_copy(c):
        return pltpu.make_async_copy(
            grad_out.at[0, :, pl.ds(pl.multiple_of(c * g_wide, LANES), g_wide)], g_buf.at[c], g_sem.at[c]
        )

    def wi_copy(c):
        return pltpu.make_async_copy(
            proj_in.at[:, pl.ds(pl.multiple_of(c * h_wide, LANES), h_wide)], wi_buf.at[c], wi_sem.at[c]
        )

    def wo_copy(c):
        return pltpu.make_async_copy(
            proj_out.at[:, pl.ds(pl.multiple_of(c * g_wide, LANES), g_wide)], wo_buf.at[c], wo_sem.at[c]
        )

    copies = [(wo_copy, g_copy, c) for c in range(g_chunks)] + [(wi_copy, h_copy, c) for c in range(h_chunks)]

    begun = [0]

    def begin(arrived):
        until = min(FIRST + 2 * arrived, arrived + AHEAD, len(copies))
        for weight, data, c in copies[begun[0]:until]:
            weight(c).start()
            data(c).start()
        begun[0] = max(begun[0], until)

    begin(0)

    barrier = pltpu.get_barrier_semaphore()
    n_all = n_dp * n_tensor

    def greet(i, carry):
        other = lax.rem(dp * n_tensor + ts + i, n_all)
        pl.semaphore_signal(
            barrier, inc=1, device_id=(other // n_tensor, lax.rem(other, n_tensor)), device_id_type=MESH
        )
        return carry

    lax.fori_loop(1, n_all, greet, 0)

    def project(group, weights, data, weight_copy, data_copy, before, panel):
        for c in group:
            weight_copy(c).wait()
            data_copy(c).wait()
            begin(before + c + 1)
        term = contract_last(weights[group[0]], data[group[0]])
        for c in group[1:]:
            term = term + contract_last(weights[c], data[c])
        if group[0] == 0:
            panel[...] = term
        else:
            panel[...] += term

    for group in groups_of(g_chunks, g_chunks, 0):
        project(group, wo_buf, g_buf, wo_copy, g_copy, 0, out_panel)

    pl.semaphore_wait(barrier, n_all - 1)

    def panel_copy(i):
        return pltpu.make_async_remote_copy(
            src_ref=out_panel,
            dst_ref=out_others.at[i - 1],
            send_sem=panel_send.at[i - 1],
            recv_sem=panel_recv.at[i - 1],
            device_id=(dp, lax.rem(ts + i, n_tensor)),
            device_id_type=MESH,
        )

    for i in range(1, n_tensor):
        panel_copy(i).start()

    in_groups = groups_of(h_chunks, h_chunks, 0)
    for group in in_groups[:-1]:
        project(group, wi_buf, h_buf, wi_copy, h_copy, g_chunks, in_panel)
    for i in range(1, n_tensor):
        panel_copy(i).wait()
    total = out_panel[...]
    for i in range(1, n_tensor):
        total = total + out_others[i - 1]
    total_parts[...] = both_parts(total)
    project(in_groups[-1], wi_buf, h_buf, wi_copy, h_copy, g_chunks, in_panel)

    width = in_panel.shape[0]
    products = contract_last(both_parts(in_panel[...]), total_parts[...])
    sums = products[:width, :width] + products[:width, width:] + products[width:, :width]
    part[...] = sums * inv_root
    even = part[pl.ds(0, width // 2, 2), :]
    odd = part[pl.ds(1, width // 2, 2), :]
    flat[...] = jnp.concatenate([even, odd], axis=1)

    def part_copy(i):
        return pltpu.make_async_remote_copy(
            src_ref=flat,
            dst_ref=flat_others.at[i - 1],
            send_sem=part_send.at[i - 1],
            recv_sem=part_recv.at[i - 1],
            device_id=(dp, lax.rem(ts + i, n_tensor)),
            device_id_type=MESH,
        )

    for i in range(1, n_tensor):
        part_copy(i).start()
    for i in range(1, n_tensor):
        part_copy(i).wait()
    grads = flat[...]
    for i in range(1, n_tensor):
        grads = grads + flat_others[i - 1]
    mine = grads[:own_rows]
    for j in range(1, n_tensor):
        mine = jnp.where(ts == j, grads[j * own_rows:(j + 1) * own_rows], mine)
    square = jnp.broadcast_to(jnp.sum(grads * grads), (1, LANES))
    for d in range(n_dp):
        message[d, :own_rows] = mine
        message[d, own_rows:own_rows + row_rows] = grads[d * row_rows:(d + 1) * row_rows]
        message[d, own_rows + row_rows:used] = square

    def message_copy(k):
        to = k + (k >= dp).astype(jnp.int32)
        slot = lax.rem(to - dp + n_dp, n_dp)
        return pltpu.make_async_remote_copy(
            src_ref=message.at[to, pl.ds(0, used)],
            dst_ref=gathered.at[slot, pl.ds(0, used)],
            send_sem=message_send.at[k],
            recv_sem=message_recv.at[slot],
            device_id=(to, ts),
            device_id_type=MESH,
        )

    for k in range(n_dp - 1):
        message_copy(k).start()
    gathered[0] = message[dp]
    for i in range(1, n_dp):
        arrived = gathered.at[i, pl.ds(0, used)]
        pltpu.make_async_copy(arrived, arrived, message_recv.at[i]).wait()
    for k in range(n_dp - 1):
        message_copy(k).wait_send()


def covariance_kernel(n_dp, n_tensor, total_len, gathered, out, block_sem, result):
    dp = lax.axis_index("dp")
    ts = lax.axis_index("tensor")
    height, wide = out.shape
    row_rows = height // LANES
    own_rows = wide // LANES
    slot = gathered.shape[0] // n_dp
    blocks, _, block = result.shape
    here = block // LANES

    def high_low(first, count):
        tiles = [gathered[pl.ds(first + k, n_dp, slot), :] for k in range(count)]
        x = jnp.concatenate(tiles, axis=1)
        high = x.astype(jnp.bfloat16).astype(jnp.float32)
        return high, x - high

    left_high, left_low = high_low(own_rows, row_rows)
    left = jnp.concatenate([left_high, left_low, left_high], axis=0) * (1.0 / n_dp)
    left = left.T.astype(jnp.bfloat16)
    squares = jnp.sum(gathered[pl.ds(own_rows + row_rows, n_dp, slot), :], axis=0, keepdims=True)
    damping = squares * (0.5 / (n_dp * total_len))
    diagonal = dp * height - ts * wide

    def block_copy(b):
        return pltpu.make_async_copy(result.at[b], out.at[:, pl.ds(b * block, block)], block_sem.at[b])

    for b in range(blocks):
        right_high, right_low = high_low(b * here, here)
        right = jnp.concatenate([right_high, right_high, right_low], axis=0).astype(jnp.bfloat16)
        result[b] = jnp.dot(left, right, preferred_element_type=jnp.float32)
        @pl.when(jnp.logical_and(diagonal >= b * block, diagonal < (b + 1) * block))
        def _():
            for r in range(row_rows):
                first = pl.multiple_of(diagonal - b * block + r * LANES, LANES)
                place = (pl.ds(r * LANES, LANES), pl.ds(first, LANES))
                ids = lax.broadcasted_iota(jnp.int32, (LANES, LANES), 0)
                same = ids == lax.broadcasted_iota(jnp.int32, (LANES, LANES), 1)
                result[(b, *place)] += jnp.where(same, damping, jnp.float32(0.0))

        block_copy(b).start()
    for b in range(blocks):
        block_copy(b).wait()


def shards(n_dp, n_tensor, hidden, grad_out, proj_in, proj_out):
    seqs_here, length, units = hidden.shape
    assert seqs_here == 1
    feats = grad_out.shape[2]
    width = proj_in.shape[0]
    total_len = width * width
    flat_rows = total_len // LANES
    own_rows = flat_rows // n_tensor
    row_rows = flat_rows // n_dp
    slot = -(-(own_rows + row_rows + 1) // 8) * 8
    h_wide, g_wide = chunk_of(units), chunk_of(feats)
    h_chunks, g_chunks = units // h_wide, feats // g_wide
    peers = max(n_tensor - 1, 1)
    f32, bf16 = jnp.float32, jnp.bfloat16
    vmem = pl.BlockSpec(memory_space=pltpu.VMEM)
    in_hbm = pl.BlockSpec(memory_space=pltpu.HBM)
    dma = pltpu.SemaphoreType.DMA
    gathered = pl.pallas_call(
        functools.partial(grads_kernel, n_dp, n_tensor, 1.0 / math.sqrt(length)),
        out_shape=jax.ShapeDtypeStruct((n_dp, slot, LANES), f32),
        in_specs=[in_hbm] * 4,
        out_specs=vmem,
        scratch_shapes=[
            pltpu.VMEM((h_chunks, length, h_wide), bf16),
            pltpu.VMEM((g_chunks, length, g_wide), bf16),
            pltpu.VMEM((h_chunks, width, h_wide), bf16),
            pltpu.VMEM((g_chunks, width, g_wide), bf16),
            pltpu.VMEM((width, length), f32),
            pltpu.VMEM((width, length), f32),
            pltpu.VMEM((peers, width, length), f32),
            pltpu.VMEM((2 * width, length), bf16),
            pltpu.VMEM((width, width), f32),
            pltpu.VMEM((flat_rows, LANES), f32),
            pltpu.VMEM((peers, flat_rows, LANES), f32),
            pltpu.VMEM((n_dp, slot, LANES), f32),
            dma((h_chunks,)),
            dma((g_chunks,)),
            dma((h_chunks,)),
            dma((g_chunks,)),
            dma((peers,)),
            dma((peers,)),
            dma((peers,)),
            dma((peers,)),
            dma((n_dp,)),
            dma((n_dp,)),
        ],
        compiler_params=pltpu.CompilerParams(
            collective_id=0, has_side_effects=True, vmem_limit_bytes=50 * 1024 * 1024
        ),
        cost_estimate=pl.CostEstimate(
            flops=2 * length * width * (units + feats),
            bytes_accessed=2 * (length + width) * (units + feats),
            transcendentals=0,
        ),
        name="projected_grads",
    )(*(pltpu.with_memory_space_constraint(x, pltpu.HBM) for x in (hidden, grad_out, proj_in, proj_out)))
    height, wide = total_len // n_dp, total_len // n_tensor
    block = min(wide, 1024)
    return pl.pallas_call(
        functools.partial(covariance_kernel, n_dp, n_tensor, total_len),
        out_shape=jax.ShapeDtypeStruct((height, wide), f32),
        in_specs=[vmem],
        out_specs=pl.BlockSpec(memory_space=pltpu.HBM),
        scratch_shapes=[dma((wide // block,)), pltpu.VMEM((wide // block, height, block), f32)],
        compiler_params=pltpu.CompilerParams(vmem_limit_bytes=16 * 1024 * 1024),
        name="covariance",
    )(gathered.reshape(n_dp * slot, LANES))


def solution(mesh):
    placed = (
        P("dp", None, "tensor"),
        P("dp", None, "tensor"),
        P(None, "tensor"),
        P(None, "tensor"),
    )
    return jax.shard_map(
        functools.partial(shards, mesh.shape["dp"], mesh.shape["tensor"]),
        mesh=mesh, in_specs=placed, out_specs=P("dp", "tensor"), check_vma=False,
    )
```

```python
import functools
import math

import jax
import jax.numpy as jnp
from jax import lax
from jax.experimental import pallas as pl
from jax.experimental.pallas import tpu as pltpu
from jax.sharding import PartitionSpec as P

MESH = pl.DeviceIdType.MESH
LANES = 128
AHEAD = 8
FIRST = 4


def chunk_of(size, largest=1024):
    best = size
    for part in range(LANES, largest + 1, LANES):
        if size % part == 0:
            best = part
    return best


def groups_of(count, first, last):
    runs, c = [], 0
    while c < count:
        size = 1 if c < first or c >= count - last or c + 1 >= count - last else 2
        runs.append(list(range(c, c + size)))
        c += size
    return runs


def both_parts(x):
    high = x.astype(jnp.bfloat16)
    low = (x - high.astype(jnp.float32)).astype(jnp.bfloat16)
    return jnp.concatenate([high, low], axis=0)


def contract_last(a, b):
    return lax.dot_general(a, b, (((1,), (1,)), ((), ())), preferred_element_type=jnp.float32)


def grads_kernel(
    n_dp, n_tensor, inv_root,
    hidden, grad_out, proj_in, proj_out,
    gathered,
    h_buf, g_buf, wi_buf, wo_buf,
    in_panel, out_panel, out_others, total_parts, part, flat, flat_others, message,
    h_sem, g_sem, wi_sem, wo_sem,
    panel_send, panel_recv, part_send, part_recv, message_send, message_recv,
):
    dp = lax.axis_index("dp")
    ts = lax.axis_index("tensor")
    h_chunks, _, h_wide = h_buf.shape
    g_chunks, _, g_wide = g_buf.shape
    flat_rows = flat.shape[0]
    own_rows = flat_rows // n_tensor
    row_rows = flat_rows // n_dp
    used = own_rows + row_rows + 1

    def h_copy(c):
        return pltpu.make_async_copy(
            hidden.at[0, :, pl.ds(pl.multiple_of(c * h_wide, LANES), h_wide)], h_buf.at[c], h_sem.at[c]
        )

    def g_copy(c):
        return pltpu.make_async_copy(
            grad_out.at[0, :, pl.ds(pl.multiple_of(c * g_wide, LANES), g_wide)], g_buf.at[c], g_sem.at[c]
        )

    def wi_copy(c):
        return pltpu.make_async_copy(
            proj_in.at[:, pl.ds(pl.multiple_of(c * h_wide, LANES), h_wide)], wi_buf.at[c], wi_sem.at[c]
        )

    def wo_copy(c):
        return pltpu.make_async_copy(
            proj_out.at[:, pl.ds(pl.multiple_of(c * g_wide, LANES), g_wide)], wo_buf.at[c], wo_sem.at[c]
        )

    copies = [(wo_copy, g_copy, c) for c in range(g_chunks)] + [(wi_copy, h_copy, c) for c in range(h_chunks)]

    begun = [0]

    def begin(arrived):
        until = min(FIRST + 2 * arrived, arrived + AHEAD, len(copies))
        for weight, data, c in copies[begun[0]:until]:
            weight(c).start()
            data(c).start()
        begun[0] = max(begun[0], until)

    begin(0)

    barrier = pltpu.get_barrier_semaphore()
    n_all = n_dp * n_tensor

    def greet(i, carry):
        other = lax.rem(dp * n_tensor + ts + i, n_all)
        pl.semaphore_signal(
            barrier, inc=1, device_id=(other // n_tensor, lax.rem(other, n_tensor)), device_id_type=MESH
        )
        return carry

    lax.fori_loop(1, n_all, greet, 0)

    def project(group, weights, data, weight_copy, data_copy, before, panel):
        for c in group:
            weight_copy(c).wait()
            data_copy(c).wait()
            begin(before + c + 1)
        term = contract_last(weights[group[0]], data[group[0]])
        for c in group[1:]:
            term = term + contract_last(weights[c], data[c])
        if group[0] == 0:
            panel[...] = term
        else:
            panel[...] += term

    for group in groups_of(g_chunks, g_chunks, 0):
        project(group, wo_buf, g_buf, wo_copy, g_copy, 0, out_panel)

    pl.semaphore_wait(barrier, n_all - 1)

    def panel_copy(i):
        return pltpu.make_async_remote_copy(
            src_ref=out_panel,
            dst_ref=out_others.at[i - 1],
            send_sem=panel_send.at[i - 1],
            recv_sem=panel_recv.at[i - 1],
            device_id=(dp, lax.rem(ts + i, n_tensor)),
            device_id_type=MESH,
        )

    for i in range(1, n_tensor):
        panel_copy(i).start()

    in_groups = groups_of(h_chunks, h_chunks, 0)
    for group in in_groups[:-1]:
        project(group, wi_buf, h_buf, wi_copy, h_copy, g_chunks, in_panel)
    for i in range(1, n_tensor):
        panel_copy(i).wait()
    total = out_panel[...]
    for i in range(1, n_tensor):
        total = total + out_others[i - 1]
    total_parts[...] = both_parts(total)
    project(in_groups[-1], wi_buf, h_buf, wi_copy, h_copy, g_chunks, in_panel)

    width = in_panel.shape[0]
    products = contract_last(both_parts(in_panel[...]), total_parts[...])
    sums = products[:width, :width] + products[:width, width:] + products[width:, :width]
    part[...] = sums * inv_root
    even = part[pl.ds(0, width // 2, 2), :]
    odd = part[pl.ds(1, width // 2, 2), :]
    flat[...] = jnp.concatenate([even, odd], axis=1)

    def part_copy(i):
        return pltpu.make_async_remote_copy(
            src_ref=flat,
            dst_ref=flat_others.at[i - 1],
            send_sem=part_send.at[i - 1],
            recv_sem=part_recv.at[i - 1],
            device_id=(dp, lax.rem(ts + i, n_tensor)),
            device_id_type=MESH,
        )

    for i in range(1, n_tensor):
        part_copy(i).start()
    for i in range(1, n_tensor):
        part_copy(i).wait()
    grads = flat[...]
    for i in range(1, n_tensor):
        grads = grads + flat_others[i - 1]
    mine = grads[:own_rows]
    for j in range(1, n_tensor):
        mine = jnp.where(ts == j, grads[j * own_rows:(j + 1) * own_rows], mine)
    square = jnp.broadcast_to(jnp.sum(grads * grads), (1, LANES))
    for d in range(n_dp):
        message[d, :own_rows] = mine
        message[d, own_rows:own_rows + row_rows] = grads[d * row_rows:(d + 1) * row_rows]
        message[d, own_rows + row_rows:used] = square

    def message_copy(k):
        to = k + (k >= dp).astype(jnp.int32)
        slot = lax.rem(to - dp + n_dp, n_dp)
        return pltpu.make_async_remote_copy(
            src_ref=message.at[to, pl.ds(0, used)],
            dst_ref=gathered.at[slot, pl.ds(0, used)],
            send_sem=message_send.at[k],
            recv_sem=message_recv.at[slot],
            device_id=(to, ts),
            device_id_type=MESH,
        )

    for k in range(n_dp - 1):
        message_copy(k).start()
    gathered[0] = message[dp]
    for i in range(1, n_dp):
        arrived = gathered.at[i, pl.ds(0, used)]
        pltpu.make_async_copy(arrived, arrived, message_recv.at[i]).wait()
    for k in range(n_dp - 1):
        message_copy(k).wait_send()


def covariance_kernel(n_dp, n_tensor, total_len, gathered, out, block_sem, result):
    dp = lax.axis_index("dp")
    ts = lax.axis_index("tensor")
    height, wide = out.shape
    row_rows = height // LANES
    own_rows = wide // LANES
    slot = gathered.shape[0] // n_dp
    blocks, _, block = result.shape
    here = block // LANES

    def high_low(first, count):
        tiles = [gathered[pl.ds(first + k, n_dp, slot), :] for k in range(count)]
        x = jnp.concatenate(tiles, axis=1)
        high = x.astype(jnp.bfloat16).astype(jnp.float32)
        return high, x - high

    left_high, left_low = high_low(own_rows, row_rows)
    left = jnp.concatenate([left_high, left_low, left_high], axis=0) * (1.0 / n_dp)
    left = left.T.astype(jnp.bfloat16)
    squares = jnp.sum(gathered[pl.ds(own_rows + row_rows, n_dp, slot), :], axis=0, keepdims=True)
    damping = squares * (0.5 / (n_dp * total_len))
    diagonal = dp * height - ts * wide

    def block_copy(b):
        return pltpu.make_async_copy(result.at[b], out.at[:, pl.ds(b * block, block)], block_sem.at[b])

    for b in range(blocks):
        right_high, right_low = high_low(b * here, here)
        right = jnp.concatenate([right_high, right_high, right_low], axis=0).astype(jnp.bfloat16)
        result[b] = jnp.dot(left, right, preferred_element_type=jnp.float32)
        @pl.when(jnp.logical_and(diagonal >= b * block, diagonal < (b + 1) * block))
        def _():
            for r in range(row_rows):
                first = pl.multiple_of(diagonal - b * block + r * LANES, LANES)
                place = (pl.ds(r * LANES, LANES), pl.ds(first, LANES))
                ids = lax.broadcasted_iota(jnp.int32, (LANES, LANES), 0)
                same = ids == lax.broadcasted_iota(jnp.int32, (LANES, LANES), 1)
                result[(b, *place)] += jnp.where(same, damping, jnp.float32(0.0))

        block_copy(b).start()
    for b in range(blocks):
        block_copy(b).wait()


def shards(n_dp, n_tensor, hidden, grad_out, proj_in, proj_out):
    seqs_here, length, units = hidden.shape
    assert seqs_here == 1
    feats = grad_out.shape[2]
    width = proj_in.shape[0]
    total_len = width * width
    flat_rows = total_len // LANES
    own_rows = flat_rows // n_tensor
    row_rows = flat_rows // n_dp
    slot = -(-(own_rows + row_rows + 1) // 8) * 8
    h_wide, g_wide = chunk_of(units), chunk_of(feats)
    h_chunks, g_chunks = units // h_wide, feats // g_wide
    peers = max(n_tensor - 1, 1)
    f32, bf16 = jnp.float32, jnp.bfloat16
    vmem = pl.BlockSpec(memory_space=pltpu.VMEM)
    in_hbm = pl.BlockSpec(memory_space=pltpu.HBM)
    dma = pltpu.SemaphoreType.DMA
    gathered = pl.pallas_call(
        functools.partial(grads_kernel, n_dp, n_tensor, 1.0 / math.sqrt(length)),
        out_shape=jax.ShapeDtypeStruct((n_dp, slot, LANES), f32),
        in_specs=[in_hbm] * 4,
        out_specs=vmem,
        scratch_shapes=[
            pltpu.VMEM((h_chunks, length, h_wide), bf16),
            pltpu.VMEM((g_chunks, length, g_wide), bf16),
            pltpu.VMEM((h_chunks, width, h_wide), bf16),
            pltpu.VMEM((g_chunks, width, g_wide), bf16),
            pltpu.VMEM((width, length), f32),
            pltpu.VMEM((width, length), f32),
            pltpu.VMEM((peers, width, length), f32),
            pltpu.VMEM((2 * width, length), bf16),
            pltpu.VMEM((width, width), f32),
            pltpu.VMEM((flat_rows, LANES), f32),
            pltpu.VMEM((peers, flat_rows, LANES), f32),
            pltpu.VMEM((n_dp, slot, LANES), f32),
            dma((h_chunks,)),
            dma((g_chunks,)),
            dma((h_chunks,)),
            dma((g_chunks,)),
            dma((peers,)),
            dma((peers,)),
            dma((peers,)),
            dma((peers,)),
            dma((n_dp,)),
            dma((n_dp,)),
        ],
        compiler_params=pltpu.CompilerParams(
            collective_id=0, has_side_effects=True, vmem_limit_bytes=50 * 1024 * 1024
        ),
        cost_estimate=pl.CostEstimate(
            flops=2 * length * width * (units + feats),
            bytes_accessed=2 * (length + width) * (units + feats),
            transcendentals=0,
        ),
        name="projected_grads",
    )(*(pltpu.with_memory_space_constraint(x, pltpu.HBM) for x in (hidden, grad_out, proj_in, proj_out)))
    height, wide = total_len // n_dp, total_len // n_tensor
    block = min(wide, 1024)
    return pl.pallas_call(
        functools.partial(covariance_kernel, n_dp, n_tensor, total_len),
        out_shape=jax.ShapeDtypeStruct((height, wide), f32),
        in_specs=[vmem],
        out_specs=pl.BlockSpec(memory_space=pltpu.HBM),
        scratch_shapes=[dma((wide // block,)), pltpu.VMEM((wide // block, height, block), f32)],
        compiler_params=pltpu.CompilerParams(vmem_limit_bytes=16 * 1024 * 1024),
        name="covariance",
    )(gathered.reshape(n_dp * slot, LANES))


def solution(mesh):
    placed = (
        P("dp", None, "tensor"),
        P("dp", None, "tensor"),
        P(None, "tensor"),
        P(None, "tensor"),
    )
    return jax.shard_map(
        functools.partial(shards, mesh.shape["dp"], mesh.shape["tensor"]),
        mesh=mesh, in_specs=placed, out_specs=P("dp", "tensor"), check_vma=False,
    )
```
